256 devices in a mesh: dom: 256 (over y, z, x, core).
Axes of the slice: x: 4, y: 4, z: 8, core: 2. Of those that a mesh axis runs over, the one named last changes fastest.
Arguments:
- thickness: float32 [80, 425984], P(None, 'dom'), may hold values from 0.5 to 2
- tracer: float32 [80, 425984], P(None, 'dom'), may hold values from -6 to 6
- velocity: float32 [80, 1277952], P(None, 'dom'), may hold values from -6 to 6
- active_levels: int32 [425984], P('dom'), may hold values from 1 to 80
- gradient_tiles: bfloat16 [9984, 2, 128, 128], P('dom'), may hold values from -0.375 to 0.375
- average_tiles: bfloat16 [9984, 2, 128, 128], P('dom'), may hold values from -0.375 to 0.375
- edge_sources: int32 [9984, 2], P('dom'), may hold values from 0 to 3327, as said below
- divergence_tiles: bfloat16 [3328, 6, 128, 128], P('dom'), may hold values from -0.21875 to 0.21875
- cell_sources: int32 [3328, 6], P('dom'), may hold values from 0 to 9983, as said below
Outputs:
- new_thickness: float32 [80, 425984], P(None, 'dom')
- new_tracer: float32 [80, 425984], P(None, 'dom')
- new_velocity: float32 [80, 1277952], P(None, 'dom')
The draws below stay inside these ranges and needn't reach their ends.
Inputs may be any that keep to these rules, and one draw needn't show every extreme that they name: `edge_sources`: entry 0 of the row of edge block e is e // 3; every other entry is e // 3 - 1 or e // 3 + 1 modulo 3328. `cell_sources`: entries 0, 1, 2 of the row of cell block b are 3b, 3b+1, 3b+2; every other entry is 3c, 3c+1 or 3c+2 with c = b - 1 or b + 1 modulo 3328.
All inputs are finite; a program needn't handle non-finite values.
Results may differ from the reference program's by a relative error of at most 0.0009.
Values may be sent and summed in bfloat16 or wider, within the bound.
No kernel may reach another device: no remote copies, remote signals or barrier semaphores. Data moves between devices by JAX's collectives and lax.ppermute only.
A program may use at most 128 MiB of HBM per device.

```python
import jax
import jax.numpy as jnp
from jax import lax

LEV = 80
TILE = 128
KG = 2
KD = 6
NBLK = 3328
NEBLK = 9984
NCELL = 425984
NEDGE = 1277952
N_DOM = 256


def draw_edge_sources(key, part):
    key = jax.random.fold_in(key, 17)
    owner = jnp.arange(3 * NBLK, dtype=jnp.int32) // 3
    sides = jax.random.randint(key, (3 * NBLK, KG - 1), 0, 2).astype(jnp.int32) * 2 - 1
    others = jnp.mod(owner[:, None] + sides, NBLK)
    return jnp.concatenate([owner[:, None], others], axis=1).astype(jnp.int32)


def draw_cell_sources(key, part):
    key = jax.random.fold_in(key, 29)
    side_key, pick_key = jax.random.split(key)
    blocks = jnp.arange(NBLK, dtype=jnp.int32)
    owned = 3 * blocks[:, None] + jnp.arange(3, dtype=jnp.int32)[None, :]
    sides = jax.random.randint(side_key, (NBLK, KD - 3), 0, 2).astype(jnp.int32) * 2 - 1
    picks = jax.random.randint(pick_key, (NBLK, KD - 3), 0, 3).astype(jnp.int32)
    others = 3 * jnp.mod(blocks[:, None] + sides, NBLK) + picks
    return jnp.concatenate([owned, others], axis=1).astype(jnp.int32)


def with_ends(values, stream_key, least, largest):
    longest = values.shape.index(max(values.shape))
    spots = []
    for shift in (0, 1):
        where = [jax.random.randint(jax.random.fold_in(stream_key, axis), (), 0, length) for axis, length in enumerate(values.shape)]
        where[longest] = (where[longest] + shift) % values.shape[longest]
        spots.append(tuple(where))
    return values.at[spots[0]].set(least).at[spots[1]].set(largest)


def block_levels(key, shape, shards, low, high):
    def one(position, parts):
        draws = jax.random.uniform(jax.random.fold_in(jax.random.fold_in(key, 6), position), (parts,), jnp.float32, low / len(shards), high / len(shards))
        return jnp.repeat(jnp.exp(draws), shape[position] // parts).reshape((-1,) + (1,) * (len(shape) - position - 1))

    loudness = one(*shards[0])
    for cut in shards[1:]:
        loudness = loudness * one(*cut)
    return loudness


def noise(own_key, shape, scale, bound, cuts=(), kind=jnp.bfloat16):
    entries = jax.random.normal(own_key, shape, jnp.float32) * scale
    if len(cuts) > 0:
        entries = block_levels(own_key, shape, cuts, -0.22, 0.18) * entries
    return jnp.clip(entries, min=-bound, max=bound).astype(kind)


def setup_inputs(seed: int = 0) -> dict:
    keys = jax.random.split(jax.random.key(seed), 10)
    return {
        "thickness": jnp.clip(0.5 + 1.5 * jax.random.uniform(keys[0], (LEV, NCELL), jnp.float32) ** block_levels(keys[0], (LEV, NCELL), ((1, 256),), -0.2, 0.2), 0.5, 2.0),
        "tracer": noise(keys[1], (LEV, NCELL), 1.0, 6.0, ((1, 256),), jnp.float32),
        "velocity": noise(keys[2], (LEV, NEDGE), 1.0, 6.0, ((1, 256),), jnp.float32),
        "active_levels": with_ends(jax.random.randint(keys[3], (NCELL,), 1, LEV + 1), jax.random.fold_in(keys[3], 1), 1, LEV).astype(jnp.int32),
        "gradient_tiles": noise(keys[4], (NEBLK, KG, TILE, TILE), (KG * TILE) ** -0.5, 0.375, ((0, 256),)),
        "average_tiles": noise(keys[5], (NEBLK, KG, TILE, TILE), (KG * TILE) ** -0.5, 0.375, ((0, 256),)),
        "edge_sources": draw_edge_sources(jax.random.fold_in(keys[9], 71), 0),
        "divergence_tiles": noise(keys[7], (NBLK, KD, TILE, TILE), (KD * TILE) ** -0.5, 0.21875, ((0, 256),)),
        "cell_sources": draw_cell_sources(jax.random.fold_in(keys[9], 71), 0),
    }


buoyancy = 0.2
drag_rate = 0.5
time_step = 0.25


def block_apply(values, tiles, sources, groups):
    height = values.shape[0]
    tile_size = tiles.shape[-1]
    blocks = values.reshape(height, -1, tile_size)
    out_blocks = tiles.shape[0]
    per_group = out_blocks // groups
    grouped_tiles = tiles.reshape((groups, per_group) + tiles.shape[1:])
    grouped_sources = sources.reshape(groups, per_group, sources.shape[1])

    def one_group(paired):
        group_tiles, group_sources = paired
        picked = blocks[:, group_sources, :].astype(jnp.float32)
        return jnp.einsum("rokc,okcf->rof", picked, group_tiles.astype(jnp.float32))

    result = lax.map(one_group, (grouped_tiles, grouped_sources))
    return jnp.transpose(result, (1, 0, 2, 3)).reshape(height, out_blocks * tile_size)


def cell_mask(active, levels):
    return (jnp.arange(levels, dtype=jnp.int32)[:, None] < active[None, :]).astype(jnp.float32)


def edge_mask(mask, tile_size):
    levels = mask.shape[0]
    per_cell = mask.reshape(levels, -1, 1, tile_size)
    return jnp.broadcast_to(per_cell, (levels, per_cell.shape[1], 3, tile_size)).reshape(levels, -1)


def pressure(thickness_now, tracer_now, mask):
    weight = thickness_now * (1.0 - buoyancy * tracer_now) * mask
    return (jnp.cumsum(weight, axis=0) - 0.5 * weight) / weight.shape[0]


def advance(anchor, current, slope, keep_share):
    return keep_share * anchor + (1.0 - keep_share) * (current + time_step * slope)


def reference(thickness, tracer, velocity, active_levels, gradient_tiles, average_tiles, edge_sources, divergence_tiles, cell_sources):
    levels = thickness.shape[0]
    tile_size = gradient_tiles.shape[-1]
    own_mask = cell_mask(active_levels, levels)
    own_edge_mask = edge_mask(own_mask, tile_size)

    def tendencies(thickness_now, tracer_now, velocity_now):
        pressures = pressure(thickness_now, tracer_now, own_mask).astype(jnp.bfloat16)
        stacked = jnp.concatenate([thickness_now, tracer_now], axis=0).astype(jnp.bfloat16)
        gradient = block_apply(pressures, gradient_tiles, edge_sources, N_DOM)
        edge_values = block_apply(stacked, average_tiles, edge_sources, N_DOM)
        d_velocity = (-gradient - drag_rate * velocity_now) * own_edge_mask
        moving = velocity_now * own_edge_mask
        fluxes = jnp.concatenate([edge_values[:levels] * moving, edge_values[levels:] * moving], axis=0).astype(jnp.bfloat16)
        spread = block_apply(fluxes, divergence_tiles, cell_sources, N_DOM)
        return (-spread[:levels] * own_mask, -spread[levels:] * own_mask, d_velocity)

    anchor = (thickness, tracer, velocity)
    keep_shares = (0.0, 0.75, 1.0 / 3.0)
    current = anchor
    for section_index in range(3):
        slopes = tendencies(current[0], current[1], current[2])
        current = tuple(advance(anchor[field], current[field], slopes[field], keep_shares[section_index]) for field in range(3))
    return (current[0], current[1], current[2])
```

```python
import jax
import jax.numpy as jnp
from jax import lax
from jax.experimental import pallas as pl
from jax.experimental.pallas import tpu as pltpu
from jax.sharding import PartitionSpec as P

buoyancy = 0.2
drag_rate = 0.5
time_step = 0.25
keep_shares = (0.0, 0.75, 1.0 / 3.0)

F32 = jnp.float32
BF16 = jnp.bfloat16
LEV = 80
TILE = 128
NEAR = 3 * LEV
NEXT = NEAR + 2 * LEV
MOVE = NEXT + 3 * LEV
SIDE = MOVE + 16


def lanes(block):
    return slice(block * TILE, (block + 1) * TILE)


def advance(anchor, current, slope, keep_share):
    if keep_share == 0.0:
        return current + time_step * slope
    return keep_share * anchor + (1.0 - keep_share) * (current + time_step * slope)


def block_mask(levels_ref, block):
    depth = lax.broadcasted_iota(jnp.int32, (LEV, TILE), 0)
    return (depth < levels_ref[0:1, lanes(block)]).astype(F32)


def above_weights():
    row = lax.broadcasted_iota(jnp.int32, (LEV, 3 * LEV), 0)
    column = lax.broadcasted_iota(jnp.int32, (LEV, 3 * LEV), 1)
    column = jnp.where(column >= 2 * LEV, column - 2 * LEV, jnp.where(column >= LEV, column - LEV, column))
    return jnp.where(column < row, 1.0, jnp.where(column == row, 0.5, 0.0)).astype(BF16)


def coded_block(thickness, tracer, mask, above):
    weight = thickness * (1.0 - buoyancy * tracer) * mask
    high = weight.astype(BF16)
    rest = weight - high.astype(F32)
    middle = rest.astype(BF16)
    low = (rest - middle.astype(F32)).astype(BF16)
    parts = jnp.concatenate([high, middle, low], axis=0)
    pressure = jnp.dot(above, parts, preferred_element_type=F32) * (1.0 / LEV)
    return jnp.concatenate([pressure.astype(BF16), thickness.astype(BF16), tracer.astype(BF16)], axis=0)


def near(offset, own, whole):
    return jnp.where(offset > own, offset - whole, jnp.where(offset < -(whole - own), offset + whole, offset))


def edge_step(levels_mask, first, second, gradient, average, velocity, anchor, keep_share):
    slope = jnp.dot(
        jnp.concatenate([first[:LEV], second[:LEV]], axis=1), gradient, preferred_element_type=F32
    )
    carried = jnp.dot(
        jnp.concatenate([first[LEV:], second[LEV:]], axis=1), average, preferred_element_type=F32
    )
    moving = velocity * levels_mask
    flux = jnp.concatenate([carried[:LEV] * moving, carried[LEV:] * moving], axis=0).astype(BF16)
    change = (-slope - drag_rate * velocity) * levels_mask
    return flux, advance(anchor, velocity, change, keep_share)


def cell_step(block, fluxes_ref, sources_ref, first_block, own, whole, tiles_ref):
    picked = []
    for t in range(6):
        offset = sources_ref[block, t] - 3 * first_block
        offset = jnp.where(offset > 3 * own + 2, offset - 3 * whole, jnp.where(offset < -3, offset + 3 * whole, offset))
        picked.append(fluxes_ref[offset + 3])
    return -jnp.dot(jnp.concatenate(picked, axis=1), tiles_ref[block], preferred_element_type=F32)


def other_block(sources_ref, edge, first_block, own, whole):
    offset = sources_ref[edge, 1] - first_block
    return jnp.where(offset > own, offset - whole, jnp.where(offset < -1, offset + whole, offset))


def start_kernel(own, thickness, tracer, velocity, levels, average, edge_sources, coded, inner, outer, staged):
    above = above_weights()
    position = lax.axis_index("dom")
    whole = own * lax.axis_size("dom")
    for block in range(own):
        mask = block_mask(levels, block)
        coded[block] = coded_block(thickness[:, lanes(block)], tracer[:, lanes(block)], mask, above)
    for side, block, after in ((0, 0, 1), (1, own - 1, own - 2)):
        mask = block_mask(levels, block)
        staged[side, 0:NEAR, :] = coded[block]
        staged[side, NEAR:NEXT, :] = coded[after, LEV:, :]
        for j in range(3):
            edge = 3 * block + j
            staged[side, NEXT + j * LEV : NEXT + (j + 1) * LEV, :] = (velocity[:, lanes(edge)] * mask).astype(BF16)
            staged[side, SIDE + j * 256 : SIDE + (j + 1) * 256, :] = average[edge]
        row = lax.broadcasted_iota(jnp.int32, (16, TILE), 0)
        signs = jnp.zeros((16, TILE), F32)
        for j in range(3):
            other = other_block(edge_sources, 3 * block + j, position * own, own, whole)
            signs = jnp.where(row == j, (other - block).astype(F32), signs)
        staged[side, MOVE:SIDE, :] = signs.astype(BF16)
    inner_side = 1 - lax.rem(position, 2)
    inner[...] = staged[inner_side]
    outer[...] = staged[1 - inner_side]


def inside_kernel(
    own, keep_share,
    coded, thickness, tracer, velocity, thickness0, tracer0, velocity0, levels,
    gradient, average, edge_sources, divergence, cell_sources,
    fluxes, new_coded, new_thickness, new_tracer, new_velocity,
):
    above = above_weights()
    position = lax.axis_index("dom")
    whole = own * lax.axis_size("dom")
    first_block = position * own

    for block in range(1, own - 1):
        mask = block_mask(levels, block)
        for edge in range(3 * block, 3 * block + 3):
            other = other_block(edge_sources, edge, first_block, own, whole)
            flux, updated = edge_step(
                mask, coded[block], coded[other], gradient[edge], average[edge],
                velocity[:, lanes(edge)], velocity0[:, lanes(edge)], keep_share,
            )
            fluxes[edge + 3] = flux
            new_velocity[:, lanes(edge)] = updated
    for block in range(2, own - 2):
        finish_cell(
            block, own, keep_share, above, first_block, whole,
            thickness, tracer, thickness0, tracer0, levels, divergence, cell_sources,
            fluxes, new_coded, new_thickness, new_tracer,
        )


def finish_cell(
    block, own, keep_share, above, first_block, whole,
    thickness, tracer, thickness0, tracer0, levels, divergence, cell_sources,
    fluxes, new_coded, new_thickness, new_tracer,
):
    at = lanes(block)
    mask = block_mask(levels, block)
    change = cell_step(block, fluxes, cell_sources, first_block, own, whole, divergence)
    h = advance(thickness0[:, at], thickness[:, at], change[:LEV] * mask, keep_share)
    s = advance(tracer0[:, at], tracer[:, at], change[LEV:] * mask, keep_share)
    new_thickness[:, at] = h
    new_tracer[:, at] = s
    if new_coded is not None:
        new_coded[block] = coded_block(h, s, mask, above)


def rim_kernel(
    own, keep_share, last,
    inner_in, outer_in, tiles_inner, tiles_outer,
    coded, thickness, tracer, velocity, thickness0, tracer0, velocity0, levels,
    gradient, average, edge_sources, divergence, cell_sources,
    fluxes_in, new_coded_in, new_thickness_in, new_tracer_in, new_velocity_in,
    fluxes, new_coded, new_thickness, new_tracer, new_velocity,
    *rest,
):
    if last:
        halo, halo_tiles = rest
    else:
        inner, outer, halo, halo_tiles, staged = rest
    above = above_weights()
    position = lax.axis_index("dom")
    whole = own * lax.axis_size("dom")
    first_block = position * own
    inner_side = 1 - lax.rem(position, 2)
    halo[inner_side] = inner_in[0:MOVE, :]
    halo[1 - inner_side] = outer_in[0:MOVE, :]
    halo_tiles[inner_side] = tiles_inner[MOVE:, :]
    halo_tiles[1 - inner_side] = tiles_outer[MOVE:, :]

    for side, block, after in ((0, 0, 1), (1, own - 1, own - 2)):
        mask = block_mask(levels, block)
        outward = 2 * side - 1
        beyond = -1 if side == 0 else own
        signs = halo_tiles[side, 0:16, :].astype(F32)
        for j in range(3):
            edge = 3 * block + j
            other = other_block(edge_sources, edge, first_block, own, whole)
            away = jnp.full((3 * LEV, TILE), (other == beyond).astype(F32))
            second = jnp.where(away > 0.5, halo[side, 0:NEAR, :].astype(F32), coded[after].astype(F32)).astype(BF16)
            flux, updated = edge_step(
                mask, coded[block], second, gradient[edge], average[edge],
                velocity[:, lanes(edge)], velocity0[:, lanes(edge)], keep_share,
            )
            fluxes[edge + 3] = flux
            new_velocity[:, lanes(edge)] = updated
            toward = signs[j : j + 1, :] * outward
            second = jnp.where(
                jnp.broadcast_to(toward, (2 * LEV, TILE)) > 0.0,
                halo[side, NEAR:NEXT, :].astype(F32),
                coded[block, LEV:, :].astype(F32),
            ).astype(BF16)
            carried = jnp.dot(
                jnp.concatenate([halo[side, LEV:NEAR, :], second], axis=1),
                halo_tiles[side, 16 + j * 256 : 16 + (j + 1) * 256, :],
                preferred_element_type=F32,
            )
            moving = halo[side, NEXT + j * LEV : NEXT + (j + 1) * LEV, :].astype(F32)
            fluxes[3 * beyond + 3 + j] = jnp.concatenate(
                [carried[:LEV] * moving, carried[LEV:] * moving], axis=0
            ).astype(BF16)
    for block in (0, 1, own - 2, own - 1):
        finish_cell(
            block, own, keep_share, above, first_block, whole,
            thickness, tracer, thickness0, tracer0, levels, divergence, cell_sources,
            fluxes, None if last else new_coded, new_thickness, new_tracer,
        )
    if not last:
        for side, block, after in ((0, 0, 1), (1, own - 1, own - 2)):
            mask = block_mask(levels, block)
            staged[side, 0:NEAR, :] = new_coded[block]
            staged[side, NEAR:NEXT, :] = new_coded[after, LEV:, :]
            for j in range(3):
                edge = 3 * block + j
                staged[side, NEXT + j * LEV : NEXT + (j + 1) * LEV, :] = (new_velocity[:, lanes(edge)] * mask).astype(BF16)
        inner[...] = staged[inner_side]
        outer[...] = staged[1 - inner_side]


def in_vmem(array):
    return pltpu.with_memory_space_constraint(array, pltpu.VMEM)


def local(
    thickness,
    tracer,
    velocity,
    active_levels,
    gradient_tiles,
    average_tiles,
    edge_sources,
    divergence_tiles,
    cell_sources,
):
    own = cell_sources.shape[0]
    devices = lax.axis_size("dom")
    within = [(i, i ^ 1) for i in range(devices)]
    across = [(i, (i + 1) % devices if i % 2 else (i - 1) % devices) for i in range(devices)]
    cells, edges = thickness.shape[1], velocity.shape[1]
    vmem = pl.BlockSpec(memory_space=pltpu.VMEM)
    smem = pl.BlockSpec(memory_space=pltpu.SMEM)
    params = pltpu.CompilerParams(vmem_limit_bytes=16 * 1024 * 1024)

    gradient = in_vmem(gradient_tiles.reshape(3 * own, 2 * TILE, TILE))
    average = in_vmem(average_tiles.reshape(3 * own, 2 * TILE, TILE))
    divergence = in_vmem(divergence_tiles.reshape(own, 6 * TILE, TILE))
    levels = in_vmem(active_levels.reshape(1, cells))
    thickness0, tracer0, velocity0 = in_vmem(thickness), in_vmem(tracer), in_vmem(velocity)
    first_rows = SIDE + 6 * TILE

    def message(rows):
        return pltpu.VMEM((rows, TILE), BF16)

    coded, inner, outer = pl.pallas_call(
        lambda *refs: start_kernel(own, *refs),
        out_shape=(pltpu.VMEM((own, NEAR, TILE), BF16), message(first_rows), message(first_rows)),
        in_specs=[vmem] * 5 + [smem],
        out_specs=[vmem] * 3,
        scratch_shapes=[pltpu.VMEM((2, first_rows, TILE), BF16)],
        compiler_params=params,
        name="start",
    )(thickness0, tracer0, velocity0, levels, average, edge_sources)

    state = (thickness0, tracer0, velocity0)
    tiles_inner = tiles_outer = None
    for section in range(3):
        last = section == 2
        keep_share = keep_shares[section]
        inner_in = lax.ppermute(inner, "dom", within)
        outer_in = lax.ppermute(outer, "dom", across)
        if section == 0:
            tiles_inner, tiles_outer = inner_in, outer_in
        common = (coded, *state, thickness0, tracer0, velocity0, levels, gradient, average, edge_sources, divergence, cell_sources)
        common_specs = [vmem] * 10 + [smem, vmem, smem]
        kind = pltpu.VMEM
        built_shapes = (
            pltpu.VMEM((3 * own + 6, 2 * LEV, TILE), BF16),
            pltpu.VMEM((own, NEAR, TILE), BF16),
            kind((LEV, cells), F32),
            kind((LEV, cells), F32),
            kind((LEV, edges), F32),
        )
        built = pl.pallas_call(
            lambda *refs, keep_share=keep_share: inside_kernel(own, keep_share, *refs),
            out_shape=built_shapes,
            in_specs=common_specs,
            out_specs=[vmem] * 5,
            compiler_params=params,
            name="inside",
        )(*common)
        built = pl.pallas_call(
            lambda *refs, keep_share=keep_share, last=last: rim_kernel(own, keep_share, last, *refs),
            out_shape=built_shapes + (() if last else (message(MOVE), message(MOVE))),
            in_specs=[vmem] * 4 + common_specs + [vmem] * 5,
            out_specs=[vmem] * (5 if last else 7),
            scratch_shapes=[pltpu.VMEM((2, MOVE, TILE), BF16), pltpu.VMEM((2, 16 + 6 * TILE, TILE), BF16)]
            + ([] if last else [pltpu.VMEM((2, MOVE, TILE), BF16)]),
            input_output_aliases={4 + len(common) + i: i for i in range(5)},
            compiler_params=params,
            name="rim",
        )(inner_in, outer_in, tiles_inner, tiles_outer, *common, *built)
        coded = built[1]
        state = built[2:5]
        if not last:
            inner, outer = built[5], built[6]
    return state


def solution(mesh):
    return jax.shard_map(
        local,
        mesh=mesh,
        in_specs=(
            P(None, "dom"),
            P(None, "dom"),
            P(None, "dom"),
            P("dom"),
            P("dom", None, None, None),
            P("dom", None, None, None),
            P("dom", None),
            P("dom", None, None, None),
            P("dom", None),
        ),
        out_specs=(P(None, "dom"), P(None, "dom"), P(None, "dom")),
        check_vma=False,
    )
```

```python
import jax
import jax.numpy as jnp
from jax import lax
from jax.experimental import pallas as pl
from jax.experimental.pallas import tpu as pltpu
from jax.sharding import PartitionSpec as P

buoyancy = 0.2
drag_rate = 0.5
time_step = 0.25
keep_shares = (0.0, 0.75, 1.0 / 3.0)

F32 = jnp.float32
BF16 = jnp.bfloat16
LEV = 80
TILE = 128
NEAR = 3 * LEV
NEXT = NEAR + 2 * LEV
MOVE = NEXT + 3 * LEV
SIDE = MOVE + 16


def lanes(block):
    return slice(block * TILE, (block + 1) * TILE)


def advance(anchor, current, slope, keep_share):
    if keep_share == 0.0:
        return current + time_step * slope
    return keep_share * anchor + (1.0 - keep_share) * (current + time_step * slope)


def block_mask(levels_ref, block):
    depth = lax.broadcasted_iota(jnp.int32, (LEV, TILE), 0)
    return (depth < levels_ref[block : block + 1, :]).astype(F32)


def above_weights():
    row = lax.broadcasted_iota(jnp.int32, (LEV, 3 * LEV), 0)
    column = lax.broadcasted_iota(jnp.int32, (LEV, 3 * LEV), 1)
    column = jnp.where(column >= 2 * LEV, column - 2 * LEV, jnp.where(column >= LEV, column - LEV, column))
    return jnp.where(column < row, 1.0, jnp.where(column == row, 0.5, 0.0)).astype(BF16)


def pressure_of(done, above):
    highs, middles, lows = [], [], []
    for thickness, tracer, mask in done:
        weight = thickness * (1.0 - buoyancy * tracer) * mask
        high = weight.astype(BF16)
        rest = weight - high.astype(F32)
        middle = rest.astype(BF16)
        highs.append(high)
        middles.append(middle)
        lows.append((rest - middle.astype(F32)).astype(BF16))
    parts = jnp.concatenate([jnp.concatenate(p, axis=1) for p in (highs, middles, lows)], axis=0)
    return jnp.dot(above, parts, preferred_element_type=F32) * (1.0 / LEV)


def code_blocks(coded, blocks, done, above):
    pressures = pressure_of(done, above)
    for i, (block, (thickness, tracer, mask)) in enumerate(zip(blocks, done)):
        coded[block, 0:LEV, :] = pressures[:, lanes(i)].astype(BF16)
        coded[block, LEV : 2 * LEV, :] = thickness.astype(BF16)
        coded[block, 2 * LEV : NEAR, :] = tracer.astype(BF16)


def edge_step(levels_mask, first, second, gradient, average, velocity, anchor, keep_share):
    slope = jnp.dot(
        jnp.concatenate([first[:LEV], second[:LEV]], axis=1), gradient, preferred_element_type=F32
    )
    carried = jnp.dot(
        jnp.concatenate([first[LEV:], second[LEV:]], axis=1), average, preferred_element_type=F32
    )
    moving = velocity * levels_mask
    flux = jnp.concatenate([carried[:LEV] * moving, carried[LEV:] * moving], axis=0).astype(BF16)
    change = (-slope - drag_rate * velocity) * levels_mask
    return flux, advance(anchor, velocity, change, keep_share)


def cell_step(block, fluxes_ref, sources_ref, first_block, own, whole, tiles_ref):
    picked = []
    for t in range(6):
        offset = sources_ref[t, block] - 3 * first_block
        offset = jnp.where(offset > 3 * own + 2, offset - 3 * whole, jnp.where(offset < -3, offset + 3 * whole, offset))
        picked.append(fluxes_ref[offset + 3])
    return -jnp.dot(jnp.concatenate(picked, axis=1), tiles_ref[block], preferred_element_type=F32)


def other_block(sources_ref, edge, first_block, own, whole):
    offset = sources_ref[1, edge] - first_block
    return jnp.where(offset > own, offset - whole, jnp.where(offset < -1, offset + whole, offset))


def start_kernel(
    own, thickness, tracer, velocity, levels, average, edge_sources, cell_sources,
    inner, outer, levels_out, edge_sources_out, cell_sources_out,
    h, s, v, flat, sems,
):
    position = lax.axis_index("dom")
    whole = own * lax.axis_size("dom")
    inner_side = 1 - lax.rem(position, 2)
    ends = []
    for p, side in ((0, inner_side), (1, 1 - inner_side)):
        block = side * (own - 1)
        ends.append((p, side, block, block + 1 - 2 * side))

    def columns(block, wide):
        return pl.ds(pl.multiple_of(block * TILE, TILE), wide)

    small = [
        pltpu.make_async_copy(levels, flat, sems.at[0]),
        pltpu.make_async_copy(edge_sources, edge_sources_out, sems.at[1]),
        pltpu.make_async_copy(cell_sources, cell_sources_out, sems.at[2]),
    ]
    fields, tiles = [], []
    for p, side, block, after in ends:
        for k, b in ((0, block), (1, after)):
            fields.append(pltpu.make_async_copy(thickness.at[:, columns(b, TILE)], h.at[p, k], sems.at[3 + 4 * p + 2 * k]))
            fields.append(pltpu.make_async_copy(tracer.at[:, columns(b, TILE)], s.at[p, k], sems.at[4 + 4 * p + 2 * k]))
        fields.append(pltpu.make_async_copy(velocity.at[:, columns(3 * block, 3 * TILE)], v.at[p], sems.at[11 + p]))
        message = (inner, outer)[p]
        rows = pl.ds(pl.multiple_of(block * 6 * TILE, 6 * TILE), 6 * TILE)
        tiles.append(pltpu.make_async_copy(average.at[rows, :], message.at[pl.ds(SIDE, 6 * TILE), :], sems.at[13 + p]))
    for copy in small + fields + tiles:
        copy.start()
    above = above_weights()
    for copy in small:
        copy.wait()
    for block in range(own):
        levels_out[block] = flat[lanes(block)]
    for copy in fields:
        copy.wait()
    done = []
    for p, side, block, after in ends:
        depth = lax.broadcasted_iota(jnp.int32, (LEV, TILE), 0)
        done.append((h[p, 0], s[p, 0], (depth < levels_out[pl.ds(block, 1), :]).astype(F32)))
    pressures = pressure_of(done, above)
    for p, side, block, after in ends:
        message = (inner, outer)[p]
        mask = done[p][2]
        message[0:LEV, :] = pressures[:, lanes(p)].astype(BF16)
        message[LEV : 2 * LEV, :] = h[p, 0].astype(BF16)
        message[2 * LEV : NEAR, :] = s[p, 0].astype(BF16)
        message[NEAR : NEAR + LEV, :] = h[p, 1].astype(BF16)
        message[NEAR + LEV : NEXT, :] = s[p, 1].astype(BF16)
        row = lax.broadcasted_iota(jnp.int32, (16, TILE), 0)
        signs = jnp.zeros((16, TILE), F32)
        for j in range(3):
            message[NEXT + j * LEV : NEXT + (j + 1) * LEV, :] = (v[p, :, lanes(j)] * mask).astype(BF16)
            low = other_block(edge_sources_out, j, position * own, own, whole)
            high = other_block(edge_sources_out, 3 * (own - 1) + j, position * own, own, whole) - (own - 1)
            signs = jnp.where(row == j, jnp.where(side == 0, low, high).astype(F32), signs)
        message[MOVE:SIDE, :] = signs.astype(BF16)
    for copy in tiles:
        copy.wait()


def load_kernel(own, keep_share, *refs):
    far = refs[:6]
    levels, edge_sources, cell_sources = refs[6:9]
    fluxes, new_coded, new_thickness, new_tracer, new_velocity, coded = refs[9:15]
    here = refs[15:21]
    sems = refs[21]
    h0, s0, v0, gradient, average, divergence = here
    cuts = ((0, 3), (3, 6), (6, 9), (9, own))

    def copies(which, cut):
        lo, hi = cut
        n = hi - lo
        if which < 2:
            at = (slice(None), pl.ds(lo * TILE, n * TILE))
        elif which == 2:
            at = (slice(None), pl.ds(3 * lo * TILE, 3 * n * TILE))
        elif which < 5:
            at = (pl.ds(3 * lo, 3 * n),)
        else:
            at = (pl.ds(lo, n),)
        return pltpu.make_async_copy(far[which].at[at], here[which].at[at], sems.at[which, cuts.index(cut)])

    for which in (0, 1):
        for cut in cuts:
            copies(which, cut).start()
    for cut in cuts:
        for which in (2, 3, 4):
            copies(which, cut).start()
    for cut in cuts:
        copies(5, cut).start()
    for which in (0, 1):
        for cut in cuts:
            copies(which, cut).wait()
    above = above_weights()
    done = [(h0[:, lanes(b)], s0[:, lanes(b)], block_mask(levels, b)) for b in range(own)]
    code_blocks(coded, range(own), done, above)

    def wait_edges(block):
        for cut in cuts:
            if block == max(cut[0], 1):
                for which in (2, 3, 4):
                    copies(which, cut).wait()

    def wait_cells(block):
        for cut in cuts:
            if block == max(cut[0], 2):
                copies(5, cut).wait()

    inside_kernel(
        own, keep_share, coded, h0, s0, v0, h0, s0, v0, levels,
        gradient, average, edge_sources, divergence, cell_sources,
        fluxes, new_coded, new_thickness, new_tracer, new_velocity,
        wait_edges=wait_edges, wait_cells=wait_cells,
    )


def last_inside_kernel(own, keep_share, *refs):
    common = refs[:13]
    fluxes, far_h, far_s, far_v, h, s, v, sems = refs[13:]
    sent = []

    def after_edges():
        at = (slice(None), pl.ds(3 * TILE, 3 * (own - 2) * TILE))
        copy = pltpu.make_async_copy(v.at[at], far_v.at[at], sems.at[0])
        copy.start()
        sent.append(copy)

    inside_kernel(own, keep_share, *common, fluxes, None, h, s, v, after_edges=after_edges)
    at = (slice(None), pl.ds(2 * TILE, (own - 4) * TILE))
    for i, (a, b) in enumerate(((h, far_h), (s, far_s))):
        copy = pltpu.make_async_copy(a.at[at], b.at[at], sems.at[1 + i])
        copy.start()
        sent.append(copy)
    for copy in sent:
        copy.wait()


def inside_kernel(
    own, keep_share,
    coded, thickness, tracer, velocity, thickness0, tracer0, velocity0, levels,
    gradient, average, edge_sources, divergence, cell_sources,
    fluxes, new_coded, new_thickness, new_tracer, new_velocity,
    wait_edges=None, wait_cells=None, after_edges=None,
):
    above = above_weights()
    position = lax.axis_index("dom")
    whole = own * lax.axis_size("dom")
    first_block = position * own

    for block in range(1, own - 1):
        if wait_edges is not None:
            wait_edges(block)
        mask = block_mask(levels, block)
        for edge in range(3 * block, 3 * block + 3):
            other = other_block(edge_sources, edge, first_block, own, whole)
            flux, updated = edge_step(
                mask, coded[block], coded[other], gradient[edge], average[edge],
                velocity[:, lanes(edge)], velocity0[:, lanes(edge)], keep_share,
            )
            fluxes[edge + 3] = flux
            new_velocity[:, lanes(edge)] = updated
    if after_edges is not None:
        after_edges()
    done = []
    for block in range(2, own - 2):
        if wait_cells is not None:
            wait_cells(block)
        done.append(
            finish_cell(
                block, own, keep_share, first_block, whole,
                thickness, tracer, thickness0, tracer0, levels, divergence, cell_sources,
                fluxes, new_thickness, new_tracer,
            )
        )
    if new_coded is not None:
        code_blocks(new_coded, range(2, own - 2), done, above)


def finish_cell(
    block, own, keep_share, first_block, whole,
    thickness, tracer, thickness0, tracer0, levels, divergence, cell_sources,
    fluxes, new_thickness, new_tracer,
):
    at = lanes(block)
    mask = block_mask(levels, block)
    change = cell_step(block, fluxes, cell_sources, first_block, own, whole, divergence)
    h = advance(thickness0[:, at], thickness[:, at], change[:LEV] * mask, keep_share)
    s = advance(tracer0[:, at], tracer[:, at], change[LEV:] * mask, keep_share)
    new_thickness[:, at] = h
    new_tracer[:, at] = s
    return h, s, mask


def rim_kernel(
    own, keep_share, last,
    inner_in, outer_in, tiles_inner, tiles_outer,
    coded, thickness, tracer, velocity, thickness0, tracer0, velocity0, levels,
    gradient, average, edge_sources, divergence, cell_sources,
    *rest,
):
    if last:
        fluxes, far_h, far_s, far_v, halo, halo_tiles, pair, new_thickness, new_tracer, new_velocity, sems = rest[4:]
    else:
        fluxes, new_coded, new_thickness, new_tracer, new_velocity = rest[5:10]
        inner, outer, halo, halo_tiles, pair, staged = rest[10:]
    above = above_weights()
    position = lax.axis_index("dom")
    whole = own * lax.axis_size("dom")
    first_block = position * own
    inner_side = 1 - lax.rem(position, 2)
    sent = []

    def send(here, far, lo, wide, sem):
        at = (slice(None), pl.ds(lo * TILE, wide * TILE))
        copy = pltpu.make_async_copy(here.at[at], far.at[at], sems.at[sem])
        copy.start()
        sent.append(copy)

    halo[inner_side] = inner_in[0:MOVE, :]
    halo[1 - inner_side] = outer_in[0:MOVE, :]
    halo_tiles[inner_side] = tiles_inner[MOVE:, :]
    halo_tiles[1 - inner_side] = tiles_outer[MOVE:, :]

    for side, block, after in ((0, 0, 1), (1, own - 1, own - 2)):
        mask = block_mask(levels, block)
        outward = 2 * side - 1
        beyond = -1 if side == 0 else own
        pair[side, 0] = halo[side, 0:NEAR, :]
        pair[side, 1] = coded[after]
        signs = halo_tiles[side, 0:16, :].astype(F32)
        for j in range(3):
            edge = 3 * block + j
            other = other_block(edge_sources, edge, first_block, own, whole)
            flux, updated = edge_step(
                mask, coded[block], pair[side, (other == after).astype(jnp.int32)], gradient[edge], average[edge],
                velocity[:, lanes(edge)], velocity0[:, lanes(edge)], keep_share,
            )
            fluxes[edge + 3] = flux
            new_velocity[:, lanes(edge)] = updated
            toward = signs[j : j + 1, :] * outward
            second = jnp.where(
                jnp.broadcast_to(toward, (2 * LEV, TILE)) > 0.0,
                halo[side, NEAR:NEXT, :].astype(F32),
                coded[block, LEV:, :].astype(F32),
            ).astype(BF16)
            carried = jnp.dot(
                jnp.concatenate([halo[side, LEV:NEAR, :], second], axis=1),
                halo_tiles[side, 16 + j * 256 : 16 + (j + 1) * 256, :],
                preferred_element_type=F32,
            )
            moving = halo[side, NEXT + j * LEV : NEXT + (j + 1) * LEV, :].astype(F32)
            fluxes[3 * beyond + 3 + j] = jnp.concatenate(
                [carried[:LEV] * moving, carried[LEV:] * moving], axis=0
            ).astype(BF16)
        if last:
            send(new_velocity, far_v, 3 * block, 3, side)
    rim = (0, 1, own - 2, own - 1)
    done = []
    for block in rim:
        done.append(
            finish_cell(
                block, own, keep_share, first_block, whole,
                thickness, tracer, thickness0, tracer0, levels, divergence, cell_sources,
                fluxes, new_thickness, new_tracer,
            )
        )
        if last and block in (1, own - 1):
            send(new_thickness, far_h, block - 1, 2, 2 if block == 1 else 3)
            send(new_tracer, far_s, block - 1, 2, 4 if block == 1 else 5)
    if last:
        for copy in sent:
            copy.wait()
    else:
        code_blocks(new_coded, rim, done, above)
        for side, block, after in ((0, 0, 1), (1, own - 1, own - 2)):
            mask = block_mask(levels, block)
            staged[side, 0:NEAR, :] = new_coded[block]
            staged[side, NEAR:NEXT, :] = new_coded[after, LEV:, :]
            for j in range(3):
                edge = 3 * block + j
                staged[side, NEXT + j * LEV : NEXT + (j + 1) * LEV, :] = (new_velocity[:, lanes(edge)] * mask).astype(BF16)
        inner[...] = staged[inner_side]
        outer[...] = staged[1 - inner_side]


def in_hbm(array):
    return pltpu.with_memory_space_constraint(array, pltpu.HBM)


def local(
    thickness,
    tracer,
    velocity,
    active_levels,
    gradient_tiles,
    average_tiles,
    edge_sources,
    divergence_tiles,
    cell_sources,
):
    own = cell_sources.shape[0]
    devices = lax.axis_size("dom")
    within = [(i, i ^ 1) for i in range(devices)]
    across = [(i, (i + 1) % devices if i % 2 else (i - 1) % devices) for i in range(devices)]
    cells, edges = thickness.shape[1], velocity.shape[1]
    vmem = pl.BlockSpec(memory_space=pltpu.VMEM)
    hbm = pl.BlockSpec(memory_space=pltpu.HBM)
    params = pltpu.CompilerParams(vmem_limit_bytes=16 * 1024 * 1024)

    gradient = in_hbm(gradient_tiles.reshape(3 * own, 2 * TILE, TILE))
    average = in_hbm(average_tiles.reshape(3 * own, 2 * TILE, TILE))
    average_rows = in_hbm(average_tiles.reshape(3 * own * 2 * TILE, TILE))
    divergence = in_hbm(divergence_tiles.reshape(own, 6 * TILE, TILE))
    thickness, tracer, velocity = in_hbm(thickness), in_hbm(tracer), in_hbm(velocity)
    first_rows = SIDE + 6 * TILE

    def message(rows):
        return pltpu.VMEM((rows, TILE), BF16)

    inner, outer, levels, edge_sources, cell_sources = pl.pallas_call(
        lambda *refs: start_kernel(own, *refs),
        out_shape=(
            message(first_rows),
            message(first_rows),
            pltpu.VMEM((own, TILE), jnp.int32),
            pltpu.VMEM((2, 3 * own), jnp.int32),
            pltpu.VMEM((6, own), jnp.int32),
        ),
        in_specs=[hbm] * 7,
        out_specs=[vmem] * 5,
        scratch_shapes=[
            pltpu.VMEM((2, 2, LEV, TILE), F32),
            pltpu.VMEM((2, 2, LEV, TILE), F32),
            pltpu.VMEM((2, LEV, 3 * TILE), F32),
            pltpu.VMEM((cells,), jnp.int32),
            pltpu.SemaphoreType.DMA((15,)),
        ],
        compiler_params=params,
        name="start",
    )(thickness, tracer, velocity, in_hbm(active_levels), average_rows, in_hbm(edge_sources.T), in_hbm(cell_sources.T))

    tiles_inner = tiles_outer = None
    state = ()
    for section in range(3):
        last = section == 2
        keep_share = keep_shares[section]
        inner_in = lax.ppermute(inner, "dom", within)
        outer_in = lax.ppermute(outer, "dom", across)
        coded_shape = pltpu.VMEM((own, NEAR, TILE), BF16)
        field_shapes = (
            pltpu.VMEM((LEV, cells), F32),
            pltpu.VMEM((LEV, cells), F32),
            pltpu.VMEM((LEV, edges), F32),
        )
        built_shapes = (pltpu.VMEM((3 * own + 6, 2 * LEV, TILE), BF16), coded_shape) + field_shapes
        if section == 0:
            tiles_inner, tiles_outer = inner_in, outer_in
            loaded = pl.pallas_call(
                lambda *refs, keep_share=keep_share: load_kernel(own, keep_share, *refs),
                out_shape=built_shapes
                + (coded_shape,)
                + field_shapes
                + (
                    pltpu.VMEM((3 * own, 2 * TILE, TILE), BF16),
                    pltpu.VMEM((3 * own, 2 * TILE, TILE), BF16),
                    pltpu.VMEM((own, 6 * TILE, TILE), BF16),
                ),
                in_specs=[hbm] * 6 + [vmem] * 3,
                out_specs=[vmem] * 12,
                scratch_shapes=[pltpu.SemaphoreType.DMA((6, 4))],
                compiler_params=params,
                name="inside",
            )(thickness, tracer, velocity, gradient, average, divergence, levels, edge_sources, cell_sources)
            built = loaded[:5]
            coded = loaded[5]
            anchor = loaded[6:9]
            gradient, average, divergence = loaded[9:]
            state = anchor
        common = (coded, *state, *anchor, levels, gradient, average, edge_sources, divergence, cell_sources)
        if last:
            built_shapes = built_shapes[:1] + (
                pltpu.HBM((LEV, cells), F32),
                pltpu.HBM((LEV, cells), F32),
                pltpu.HBM((LEV, edges), F32),
            )
        built_specs = [vmem] + [hbm] * 3 if last else [vmem] * 5
        field_scratch = list(field_shapes)
        if section > 0:
            body = last_inside_kernel if last else inside_kernel
            built = pl.pallas_call(
                lambda *refs, keep_share=keep_share, body=body: body(own, keep_share, *refs),
                out_shape=built_shapes,
                in_specs=[vmem] * 13,
                out_specs=built_specs,
                scratch_shapes=field_scratch + [pltpu.SemaphoreType.DMA((3,))] if last else [],
                compiler_params=params,
                name="inside",
            )(*common)
        scratch = [
            pltpu.VMEM((2, MOVE, TILE), BF16),
            pltpu.VMEM((2, 16 + 6 * TILE, TILE), BF16),
            pltpu.VMEM((2, 2, NEAR, TILE), BF16),
        ]
        if last:
            scratch += field_scratch + [pltpu.SemaphoreType.DMA((6,))]
        else:
            scratch += [pltpu.VMEM((2, MOVE, TILE), BF16)]
        built = pl.pallas_call(
            lambda *refs, keep_share=keep_share, last=last: rim_kernel(own, keep_share, last, *refs),
            out_shape=built_shapes + (() if last else (message(MOVE), message(MOVE))),
            in_specs=[vmem] * 17 + built_specs,
            out_specs=built_specs + ([] if last else [vmem] * 2),
            scratch_shapes=scratch,
            input_output_aliases={17 + i: i for i in range(len(built_shapes))},
            compiler_params=params,
            name="rim",
        )(inner_in, outer_in, tiles_inner, tiles_outer, *common, *built)
        if last:
            return built[1:4]
        coded = built[1]
        state = built[2:5]
        inner, outer = built[5:]


def solution(mesh):
    return jax.shard_map(
        local,
        mesh=mesh,
        in_specs=(
            P(None, "dom"),
            P(None, "dom"),
            P(None, "dom"),
            P("dom"),
            P("dom", None, None, None),
            P("dom", None, None, None),
            P("dom", None),
            P("dom", None, None, None),
            P("dom", None),
        ),
        out_specs=(P(None, "dom"), P(None, "dom"), P(None, "dom")),
        check_vma=False,
    )
```

```python
import jax
import jax.numpy as jnp
from jax import lax
from jax.experimental import pallas as pl
from jax.experimental.pallas import tpu as pltpu
from jax.sharding import PartitionSpec as P

buoyancy = 0.2
drag_rate = 0.5
time_step = 0.25
keep_shares = (0.0, 0.75, 1.0 / 3.0)

F32 = jnp.float32
BF16 = jnp.bfloat16
LEV = 80
TILE = 128
SMALL = pl.CostEstimate(flops=1000, bytes_accessed=1000, transcendentals=0)
LARGE = pl.CostEstimate(flops=10**9, bytes_accessed=10**6, transcendentals=0)
NEAR = 3 * LEV
NEXT = NEAR + 2 * LEV
MOVE = NEXT + 3 * LEV
SIDE = MOVE + 16


def lanes(block):
    return slice(block * TILE, (block + 1) * TILE)


def advance(anchor, current, slope, keep_share):
    if keep_share == 0.0:
        return current + time_step * slope
    return keep_share * anchor + (1.0 - keep_share) * (current + time_step * slope)


def block_mask(levels_ref, block):
    depth = lax.broadcasted_iota(jnp.int32, (LEV, TILE), 0)
    return (depth < levels_ref[block : block + 1, :]).astype(F32)


def above_weights():
    row = lax.broadcasted_iota(jnp.int32, (LEV, 3 * LEV), 0)
    column = lax.broadcasted_iota(jnp.int32, (LEV, 3 * LEV), 1)
    column = jnp.where(column >= 2 * LEV, column - 2 * LEV, jnp.where(column >= LEV, column - LEV, column))
    return jnp.where(column < row, 1.0, jnp.where(column == row, 0.5, 0.0)).astype(BF16)


def pressure_of(done, above):
    highs, middles, lows = [], [], []
    for thickness, tracer, mask in done:
        weight = thickness * (1.0 - buoyancy * tracer) * mask
        high = weight.astype(BF16)
        rest = weight - high.astype(F32)
        middle = rest.astype(BF16)
        highs.append(high)
        middles.append(middle)
        lows.append((rest - middle.astype(F32)).astype(BF16))
    parts = jnp.concatenate([jnp.concatenate(p, axis=1) for p in (highs, middles, lows)], axis=0)
    return jnp.dot(above, parts, preferred_element_type=F32) * (1.0 / LEV)


def code_blocks(coded, blocks, done, above):
    pressures = pressure_of(done, above)
    for i, (block, (thickness, tracer, mask)) in enumerate(zip(blocks, done)):
        coded[block, 0:LEV, :] = pressures[:, lanes(i)].astype(BF16)
        coded[block, LEV : 2 * LEV, :] = thickness.astype(BF16)
        coded[block, 2 * LEV : NEAR, :] = tracer.astype(BF16)


def edge_step(levels_mask, first, second, gradient, average, velocity, anchor, keep_share):
    slope = jnp.dot(
        jnp.concatenate([first[:LEV], second[:LEV]], axis=1), gradient, preferred_element_type=F32
    )
    carried = jnp.dot(
        jnp.concatenate([first[LEV:], second[LEV:]], axis=1), average, preferred_element_type=F32
    )
    moving = velocity * levels_mask
    flux = jnp.concatenate([carried[:LEV] * moving, carried[LEV:] * moving], axis=0).astype(BF16)
    change = (-slope - drag_rate * velocity) * levels_mask
    return flux, advance(anchor, velocity, change, keep_share)


def cell_step(block, fluxes_ref, sources_ref, first_block, own, whole, tiles_ref):
    picked = []
    for t in range(6):
        offset = sources_ref[t, block] - 3 * first_block
        offset = jnp.where(offset > 3 * own + 2, offset - 3 * whole, jnp.where(offset < -3, offset + 3 * whole, offset))
        picked.append(fluxes_ref[offset + 3])
    return -jnp.dot(jnp.concatenate(picked, axis=1), tiles_ref[block], preferred_element_type=F32)


def other_block(sources_ref, edge, first_block, own, whole):
    offset = sources_ref[1, edge] - first_block
    return jnp.where(offset > own, offset - whole, jnp.where(offset < -1, offset + whole, offset))


def start_kernel(
    own, thickness, tracer, velocity, levels, average, edge_sources, cell_sources,
    inner, outer, levels_out, edge_sources_out, cell_sources_out,
    h, s, v, flat, sems,
):
    position = lax.axis_index("dom")
    whole = own * lax.axis_size("dom")
    inner_side = 1 - lax.rem(position, 2)
    ends = []
    for p, side in ((0, inner_side), (1, 1 - inner_side)):
        block = side * (own - 1)
        ends.append((p, side, block, block + 1 - 2 * side))

    def columns(block, wide):
        return pl.ds(pl.multiple_of(block * TILE, TILE), wide)

    small = [
        pltpu.make_async_copy(levels, flat, sems.at[0]),
        pltpu.make_async_copy(edge_sources, edge_sources_out, sems.at[1]),
        pltpu.make_async_copy(cell_sources, cell_sources_out, sems.at[2]),
    ]
    fields, tiles = [], []
    for p, side, block, after in ends:
        for k, b in ((0, block), (1, after)):
            fields.append(pltpu.make_async_copy(thickness.at[:, columns(b, TILE)], h.at[p, k], sems.at[3 + 4 * p + 2 * k]))
            fields.append(pltpu.make_async_copy(tracer.at[:, columns(b, TILE)], s.at[p, k], sems.at[4 + 4 * p + 2 * k]))
        fields.append(pltpu.make_async_copy(velocity.at[:, columns(3 * block, 3 * TILE)], v.at[p], sems.at[11 + p]))
        message = (inner, outer)[p]
        rows = pl.ds(pl.multiple_of(block * 6 * TILE, 6 * TILE), 6 * TILE)
        tiles.append(pltpu.make_async_copy(average.at[rows, :], message.at[pl.ds(SIDE, 6 * TILE), :], sems.at[13 + p]))
    for copy in small + fields + tiles:
        copy.start()
    above = above_weights()
    for copy in small:
        copy.wait()
    for block in range(own):
        levels_out[block] = flat[lanes(block)]
    for copy in fields:
        copy.wait()
    done = []
    for p, side, block, after in ends:
        depth = lax.broadcasted_iota(jnp.int32, (LEV, TILE), 0)
        done.append((h[p, 0], s[p, 0], (depth < levels_out[pl.ds(block, 1), :]).astype(F32)))
    pressures = pressure_of(done, above)
    for p, side, block, after in ends:
        message = (inner, outer)[p]
        mask = done[p][2]
        message[0:LEV, :] = pressures[:, lanes(p)].astype(BF16)
        message[LEV : 2 * LEV, :] = h[p, 0].astype(BF16)
        message[2 * LEV : NEAR, :] = s[p, 0].astype(BF16)
        message[NEAR : NEAR + LEV, :] = h[p, 1].astype(BF16)
        message[NEAR + LEV : NEXT, :] = s[p, 1].astype(BF16)
        row = lax.broadcasted_iota(jnp.int32, (16, TILE), 0)
        signs = jnp.zeros((16, TILE), F32)
        for j in range(3):
            message[NEXT + j * LEV : NEXT + (j + 1) * LEV, :] = (v[p, :, lanes(j)] * mask).astype(BF16)
            low = other_block(edge_sources_out, j, position * own, own, whole)
            high = other_block(edge_sources_out, 3 * (own - 1) + j, position * own, own, whole) - (own - 1)
            signs = jnp.where(row == j, jnp.where(side == 0, low, high).astype(F32), signs)
        message[MOVE:SIDE, :] = signs.astype(BF16)
    for copy in tiles:
        copy.wait()


def first_inside(
    own, keep_share, h0, s0, v0, levels, gradient, average, edge_sources, divergence, cell_sources,
    fluxes, new_coded, new_thickness, new_tracer, new_velocity, coded,
):
    done = [(h0[:, lanes(b)], s0[:, lanes(b)], block_mask(levels, b)) for b in range(own)]
    code_blocks(coded, range(own), done, above_weights())
    inside_edges(own, keep_share, coded, v0, v0, levels, gradient, average, edge_sources, fluxes, new_velocity)
    inside_cells(
        own, keep_share, fluxes, h0, s0, h0, s0, levels, divergence, cell_sources,
        new_coded, new_thickness, new_tracer,
    )


def on(odd, work):
    pl.when(lax.rem(lax.axis_index("dom"), 2) == (1 if odd else 0))(work)


def odd_inside(
    own, keep_share, coded, velocity, velocity0, levels, gradient, average, edge_sources,
    thickness, tracer, thickness0, tracer0, divergence, cell_sources,
    fluxes, new_velocity, new_thickness, new_tracer,
):
    def work():
        inside_edges(
            own, keep_share, coded, velocity, velocity0, levels, gradient, average, edge_sources, fluxes, new_velocity
        )
        inside_cells(
            own, keep_share, fluxes, thickness, tracer, thickness0, tracer0, levels, divergence, cell_sources,
            None, new_thickness, new_tracer,
        )

    on(True, work)


def even_edges(own, keep_share, *refs):
    on(False, lambda: inside_edges(own, keep_share, *refs[:7], *refs[9:]))


def even_cells(own, keep_share, *refs):
    on(False, lambda: inside_cells(own, keep_share, *refs[:8], None, *refs[10:]))


def tick(own, keep_share, *refs):
    pass


def inside_edges(
    own, keep_share, coded, velocity, velocity0, levels, gradient, average, edge_sources, fluxes, new_velocity,
    wait=None,
):
    whole = own * lax.axis_size("dom")
    first_block = lax.axis_index("dom") * own
    for block in range(1, own - 1):
        if wait is not None:
            wait(block)
        mask = block_mask(levels, block)
        for edge in range(3 * block, 3 * block + 3):
            other = other_block(edge_sources, edge, first_block, own, whole)
            flux, updated = edge_step(
                mask, coded[block], coded[other], gradient[edge], average[edge],
                velocity[:, lanes(edge)], velocity0[:, lanes(edge)], keep_share,
            )
            fluxes[edge + 3] = flux
            new_velocity[:, lanes(edge)] = updated


def inside_cells(
    own, keep_share, fluxes, thickness, tracer, thickness0, tracer0, levels, divergence, cell_sources,
    new_coded, new_thickness, new_tracer, wait=None,
):
    whole = own * lax.axis_size("dom")
    first_block = lax.axis_index("dom") * own
    done = []
    for block in range(2, own - 2):
        if wait is not None:
            wait(block)
        done.append(
            finish_cell(
                block, own, keep_share, first_block, whole,
                thickness, tracer, thickness0, tracer0, levels, divergence, cell_sources,
                fluxes, new_thickness, new_tracer,
            )
        )
    if new_coded is not None:
        code_blocks(new_coded, range(2, own - 2), done, above_weights())


def finish_cell(
    block, own, keep_share, first_block, whole,
    thickness, tracer, thickness0, tracer0, levels, divergence, cell_sources,
    fluxes, new_thickness, new_tracer,
):
    at = lanes(block)
    mask = block_mask(levels, block)
    change = cell_step(block, fluxes, cell_sources, first_block, own, whole, divergence)
    h = advance(thickness0[:, at], thickness[:, at], change[:LEV] * mask, keep_share)
    s = advance(tracer0[:, at], tracer[:, at], change[LEV:] * mask, keep_share)
    new_thickness[:, at] = h
    new_tracer[:, at] = s
    return h, s, mask


def rim_step(
    odd, own, keep_share, last,
    outer_in, inner_in, tiles_outer, tiles_inner,
    coded, thickness, tracer, velocity, thickness0, tracer0, velocity0, levels,
    gradient, average, edge_sources, divergence, cell_sources,
    fluxes, new_coded, new_thickness, new_tracer, new_velocity, pair,
    inner, outer, send,
):
    above = above_weights()
    first_block = lax.axis_index("dom") * own
    whole = own * lax.axis_size("dom")
    halos = (inner_in, outer_in) if odd else (outer_in, inner_in)
    halo_tiles = (tiles_inner, tiles_outer) if odd else (tiles_outer, tiles_inner)
    messages = (inner, outer) if odd else (outer, inner)
    ends = ((0, 0, 1), (1, own - 1, own - 2))

    for side, block, after in ends:
        mask = block_mask(levels, block)
        outward = 2 * side - 1
        beyond = -1 if side == 0 else own
        halo, tiles = halos[side], halo_tiles[side]
        pair[side, 0] = halo[0:NEAR, :]
        pair[side, 1] = coded[after]
        signs = tiles[MOVE:SIDE, :].astype(F32)
        for j in range(3):
            edge = 3 * block + j
            other = other_block(edge_sources, edge, first_block, own, whole)
            flux, updated = edge_step(
                mask, coded[block], pair[side, (other == after).astype(jnp.int32)], gradient[edge], average[edge],
                velocity[:, lanes(edge)], velocity0[:, lanes(edge)], keep_share,
            )
            fluxes[edge + 3] = flux
            new_velocity[:, lanes(edge)] = updated
            toward = signs[j : j + 1, :] * outward
            second = jnp.where(
                jnp.broadcast_to(toward, (2 * LEV, TILE)) > 0.0,
                halo[NEAR:NEXT, :].astype(F32),
                coded[block, LEV:, :].astype(F32),
            ).astype(BF16)
            carried = jnp.dot(
                jnp.concatenate([halo[LEV:NEAR, :], second], axis=1),
                tiles[SIDE + j * 256 : SIDE + (j + 1) * 256, :],
                preferred_element_type=F32,
            )
            moving = halo[NEXT + j * LEV : NEXT + (j + 1) * LEV, :].astype(F32)
            fluxes[3 * beyond + 3 + j] = jnp.concatenate(
                [carried[:LEV] * moving, carried[LEV:] * moving], axis=0
            ).astype(BF16)
            if not last:
                messages[side][NEXT + j * LEV : NEXT + (j + 1) * LEV, :] = (updated * mask).astype(BF16)
        if last:
            send(2, 3 * block, 3)
    rim = (0, 1, own - 2, own - 1)
    done = []
    for block in rim:
        done.append(
            finish_cell(
                block, own, keep_share, first_block, whole,
                thickness, tracer, thickness0, tracer0, levels, divergence, cell_sources,
                fluxes, new_thickness, new_tracer,
            )
        )
        if last and block in (1, own - 1):
            send(0, block - 1, 2)
            send(1, block - 1, 2)
    if last:
        return
    code_blocks(new_coded, rim, done, above)
    for side, block, after in ends:
        messages[side][0:NEAR, :] = new_coded[block]
        messages[side][NEAR:NEXT, :] = new_coded[after, LEV:, :]


def rim_kernel(odd, second, own, keep_share, *refs):
    common = refs[:17]
    out = refs[17 + 5 + (1 if second else 0) :]
    built, inner, outer, pair = out[:5], out[5], out[6], out[7]

    @pl.when(lax.rem(lax.axis_index("dom"), 2) == (1 if odd else 0))
    def _():
        rim_step(odd, own, keep_share, False, *common, *built, pair, inner, outer, None)


def last_rim_kernel(own, keep_share, *refs):
    inner_in, up_in, down_in, tiles_inner, tiles_up, tiles_down = refs[:6]
    common = refs[6:19]
    fluxes, h, s, v, far_h, far_s, far_v, pair, sems = refs[23:]
    here, far = (h, s, v), (far_h, far_s, far_v)
    odd_here = lax.rem(lax.axis_index("dom"), 2)
    whole = []
    for which in (2, 0, 1):
        lo, wide = (3, 3 * (own - 2)) if which == 2 else (2, own - 4)
        at = (slice(None), pl.ds(lo * TILE, wide * TILE))
        whole.append(pltpu.make_async_copy(here[which].at[at], far[which].at[at], sems.at[which]))
        whole[-1].start()

    for odd in (False, True):

        @pl.when(odd_here == (1 if odd else 0))
        def _(odd=odd):
            sent = []

            def send(which, lo, wide):
                at = (slice(None), pl.ds(lo * TILE, wide * TILE))
                copy = pltpu.make_async_copy(here[which].at[at], far[which].at[at], sems.at[3 + len(sent)])
                copy.start()
                sent.append(copy)

            rim_step(
                odd, own, keep_share, True,
                down_in if odd else up_in, inner_in, tiles_down if odd else tiles_up, tiles_inner,
                *common, fluxes, None, h, s, v, pair, None, None, send,
            )
            for copy in sent:
                copy.wait()

    for copy in whole:
        copy.wait()


def in_vmem(array):
    return pltpu.with_memory_space_constraint(array, pltpu.VMEM)


def in_hbm(array):
    return pltpu.with_memory_space_constraint(array, pltpu.HBM)


def local(
    thickness,
    tracer,
    velocity,
    active_levels,
    gradient_tiles,
    average_tiles,
    edge_sources,
    divergence_tiles,
    cell_sources,
):
    own = cell_sources.shape[0]
    devices = lax.axis_size("dom")
    within = [(i, i ^ 1) for i in range(devices)]
    upward = [(i, (i + 1) % devices) for i in range(devices)]
    filler = {1: 1, 3: -3, 5: -1, 7: -1}
    downward = [(i, (i + filler[i % 8]) % devices if i % 2 else (i - 1) % devices) for i in range(devices)]
    cells, edges = thickness.shape[1], velocity.shape[1]
    vmem = pl.BlockSpec(memory_space=pltpu.VMEM)
    hbm = pl.BlockSpec(memory_space=pltpu.HBM)
    params = pltpu.CompilerParams(vmem_limit_bytes=16 * 1024 * 1024)

    gradient = (gradient_tiles.reshape(3 * own, 2 * TILE, TILE))
    average = (average_tiles.reshape(3 * own, 2 * TILE, TILE))
    average_rows = in_hbm(average_tiles.reshape(3 * own * 2 * TILE, TILE))
    divergence = (divergence_tiles.reshape(own, 6 * TILE, TILE))
    first_rows = SIDE + 6 * TILE

    def message(rows):
        return pltpu.VMEM((rows, TILE), BF16)

    inner, outer, levels, edge_sources, cell_sources = pl.pallas_call(
        lambda *refs: start_kernel(own, *refs),
        out_shape=(
            message(first_rows),
            message(first_rows),
            pltpu.VMEM((own, TILE), jnp.int32),
            pltpu.VMEM((2, 3 * own), jnp.int32),
            pltpu.VMEM((6, own), jnp.int32),
        ),
        in_specs=[hbm] * 7,
        out_specs=[vmem] * 5,
        scratch_shapes=[
            pltpu.VMEM((2, 2, LEV, TILE), F32),
            pltpu.VMEM((2, 2, LEV, TILE), F32),
            pltpu.VMEM((2, LEV, 3 * TILE), F32),
            pltpu.VMEM((cells,), jnp.int32),
            pltpu.SemaphoreType.DMA((15,)),
        ],
        compiler_params=params,
        cost_estimate=pl.CostEstimate(flops=2 * 10**10, bytes_accessed=10**6, transcendentals=0),
        name="start",
    )(in_hbm(thickness), in_hbm(tracer), in_hbm(velocity), in_hbm(active_levels), average_rows, in_hbm(edge_sources.T), in_hbm(cell_sources.T))

    coded_shape = pltpu.VMEM((own, NEAR, TILE), BF16)
    field_shapes = (
        pltpu.VMEM((LEV, cells), F32),
        pltpu.VMEM((LEV, cells), F32),
        pltpu.VMEM((LEV, edges), F32),
    )
    flux_shape = pltpu.VMEM((3 * own + 6, 2 * LEV, TILE), BF16)
    built_shapes = (flux_shape, coded_shape) + field_shapes
    pair_scratch = pltpu.VMEM((2, 2, NEAR, TILE), BF16)

    def send_up(x):
        return lax.ppermute(x, "dom", upward)

    def send_down(x):
        return lax.ppermute(x, "dom", downward)

    def swap_inner(x):
        return lax.ppermute(x, "dom", within)

    def rim(odd, keep_share, inner_in, outer_in, tiles_outer, common, built, inner):
        second = inner is not None
        extra = (inner,) if second else ()
        out = pl.pallas_call(
            lambda *refs: rim_kernel(odd, second, own, keep_share, *refs),
            out_shape=built_shapes + (message(MOVE), message(MOVE)),
            in_specs=[vmem] * (17 + 5 + len(extra)),
            out_specs=[vmem] * 7,
            scratch_shapes=[pair_scratch],
            input_output_aliases={17 + i: i for i in range(5 + len(extra))},
            compiler_params=params,
            cost_estimate=LARGE,
            name="rim_odd" if odd else "rim_even",
        )(outer_in, inner_in, tiles_outer, tiles_inner, *common, *built, *extra)
        return out[:5], out[5], out[6]

    def call(body, keep_share, operands, shapes, specs, scratch, name, after=None, passed=None, filled=()):
        n = len(operands)
        extra = tuple(x for x in (after, passed) if x is not None)
        given = tuple(x for x in (passed,) if x is not None) + filled
        total = n + len(extra) + len(filled)
        first = 0 if passed is None else 1
        return pl.pallas_call(
            lambda *refs: body(own, keep_share, *refs[:n], *refs[n + len(extra) : total], *refs[total + first :]),
            out_shape=tuple(pltpu.VMEM(x.shape, x.dtype) for x in given) + shapes,
            in_specs=[vmem] * total,
            out_specs=[vmem] * len(given) + specs,
            input_output_aliases={total - len(given) + i: i for i in range(len(given))},
            scratch_shapes=scratch,
            compiler_params=params,
            cost_estimate=SMALL,
            name=name,
        )(*operands, *extra, *filled)

    def edges_inside(keep_share, common, passed=None):
        operands = (common[0], common[3], common[6], *common[7:11])
        shapes = (flux_shape, field_shapes[2])
        return call(inside_edges, keep_share, operands, shapes, [vmem] * 2, [], "inside_edges", passed=passed)

    def cell_operands(fluxes, common):
        return (fluxes, common[1], common[2], common[4], common[5], common[7], common[11], common[12])

    up_in, down_in = lax.ppermute(outer, "dom", upward), lax.ppermute(outer, "dom", [(j, i) for i, j in upward])
    anchor = (in_vmem(thickness), in_vmem(tracer), in_vmem(velocity))
    gradient, average, divergence = in_vmem(gradient), in_vmem(average), in_vmem(divergence)
    loaded = call(
        first_inside, keep_shares[0],
        (*anchor, levels, gradient, average, edge_sources, divergence, cell_sources),
        built_shapes + (coded_shape,), [vmem] * 6, [], "inside",
    )
    built, coded = loaded[:5], loaded[5]
    inner_in = swap_inner(inner)
    tiles_up, tiles_down, tiles_inner = up_in, down_in, inner_in

    def operands(coded, state):
        return (coded, *state, *anchor, levels, gradient, average, edge_sources, divergence, cell_sources)

    common = operands(coded, anchor)
    built, inner, outer = rim(False, keep_shares[0], inner_in, up_in, tiles_up, common, built, None)
    next_down = send_down(outer)
    built, inner, outer = rim(True, keep_shares[0], inner_in, down_in, tiles_down, common, built, inner)
    next_up = send_up(outer)
    up_in, down_in, inner_in = next_up, next_down, swap_inner(inner)

    common = operands(built[1], built[2:5])
    fluxes, new_velocity = edges_inside(keep_shares[1], common)
    new_cells = call(
        inside_cells, keep_shares[1], cell_operands(fluxes, common), (coded_shape,) + field_shapes[:2],
        [vmem] * 3, [], "inside_cells", after=down_in,
    )
    built = (fluxes, *new_cells, new_velocity)
    built, inner, outer = rim(True, keep_shares[1], inner_in, down_in, tiles_down, common, built, None)
    next_up = send_up(outer)
    built, inner, outer = rim(False, keep_shares[1], inner_in, up_in, tiles_up, common, built, inner)
    up_in, down_in = next_up, send_down(outer)

    common = operands(built[1], built[2:5])
    far_shapes = (pltpu.HBM((LEV, cells), F32), pltpu.HBM((LEV, cells), F32), pltpu.HBM((LEV, edges), F32))
    edge_operands = (common[0], common[3], common[6], *common[7:11])
    inner, fluxes, new_velocity, h, s = call(
        odd_inside, keep_shares[2],
        edge_operands + (common[1], common[2], common[4], common[5], common[11], common[12]),
        (flux_shape, field_shapes[2]) + field_shapes[:2], [vmem] * 4, [], "odd_inside", passed=inner,
    )
    inner_in = swap_inner(inner)
    fluxes = call(tick, 0.0, (up_in,), (), [], [], "tick", passed=fluxes)[0]
    fluxes, new_velocity = call(
        even_edges, keep_shares[2], edge_operands, (), [], [], "even_edges", filled=(fluxes, new_velocity)
    )
    h, s = call(
        even_cells, keep_shares[2], cell_operands(fluxes, common), (), [], [], "even_cells", filled=(h, s)
    )
    results = pl.pallas_call(
        lambda *refs: last_rim_kernel(own, keep_shares[2], *refs),
        out_shape=(flux_shape,) + field_shapes + far_shapes,
        in_specs=[vmem] * 23,
        out_specs=[vmem] * 4 + [hbm] * 3,
        scratch_shapes=[pair_scratch, pltpu.SemaphoreType.DMA((9,))],
        input_output_aliases={19 + i: i for i in range(4)},
        compiler_params=params,
        cost_estimate=SMALL,
        name="rim",
    )(inner_in, up_in, down_in, tiles_inner, tiles_up, tiles_down, *common, fluxes, h, s, new_velocity)
    return results[4:]


def solution(mesh):
    return jax.shard_map(
        local,
        mesh=mesh,
        in_specs=(
            P(None, "dom"),
            P(None, "dom"),
            P(None, "dom"),
            P("dom"),
            P("dom", None, None, None),
            P("dom", None, None, None),
            P("dom", None),
            P("dom", None, None, None),
            P("dom", None),
        ),
        out_specs=(P(None, "dom"), P(None, "dom"), P(None, "dom")),
        check_vma=False,
    )
```

```python
import functools

import jax
import jax.numpy as jnp
from jax import lax
from jax.experimental import pallas as pl
from jax.experimental.pallas import tpu as pltpu
from jax.sharding import PartitionSpec as P

buoyancy = 0.2
drag_rate = 0.5
time_step = 0.25
keep_shares = (0.0, 0.75, 1.0 / 3.0)

F32 = jnp.float32
BF16 = jnp.bfloat16
LEV = 80
EVEN = (0, 2, 4, 6)
TILE = 128
SMALL = pl.CostEstimate(flops=1000, bytes_accessed=1000, transcendentals=0)
LARGE = pl.CostEstimate(flops=10**9, bytes_accessed=10**6, transcendentals=0)
NEAR = 3 * LEV
NEXT = NEAR + 2 * LEV
MOVE = NEXT + 3 * LEV
SIDE = MOVE + 16


def lanes(block):
    return slice(block * TILE, (block + 1) * TILE)


def advance(anchor, current, slope, keep_share):
    if keep_share == 0.0:
        return current + time_step * slope
    return keep_share * anchor + (1.0 - keep_share) * (current + time_step * slope)


def block_mask(levels_ref, block):
    depth = lax.broadcasted_iota(jnp.int32, (LEV, TILE), 0)
    return (depth < levels_ref[block : block + 1, :]).astype(F32)


def above_weights():
    row = lax.broadcasted_iota(jnp.int32, (LEV, 3 * LEV), 0)
    column = lax.broadcasted_iota(jnp.int32, (LEV, 3 * LEV), 1)
    column = jnp.where(column >= 2 * LEV, column - 2 * LEV, jnp.where(column >= LEV, column - LEV, column))
    return jnp.where(column < row, 1.0, jnp.where(column == row, 0.5, 0.0)).astype(BF16)


def pressure_of(done, above):
    highs, middles, lows = [], [], []
    for thickness, tracer, mask in done:
        weight = thickness * (1.0 - buoyancy * tracer) * mask
        high = weight.astype(BF16)
        rest = weight - high.astype(F32)
        middle = rest.astype(BF16)
        highs.append(high)
        middles.append(middle)
        lows.append((rest - middle.astype(F32)).astype(BF16))
    parts = jnp.concatenate([jnp.concatenate(p, axis=1) for p in (highs, middles, lows)], axis=0)
    return jnp.dot(above, parts, preferred_element_type=F32) * (1.0 / LEV)


def code_blocks(coded, blocks, done, above):
    pressures = pressure_of(done, above)
    for i, (block, (thickness, tracer, mask)) in enumerate(zip(blocks, done)):
        coded[block, 0:LEV, :] = pressures[:, lanes(i)].astype(BF16)
        coded[block, LEV : 2 * LEV, :] = thickness.astype(BF16)
        coded[block, 2 * LEV : NEAR, :] = tracer.astype(BF16)


def edge_step(levels_mask, first, second, gradient, average, velocity, anchor, keep_share):
    slope = jnp.dot(
        jnp.concatenate([first[:LEV], second[:LEV]], axis=1), gradient, preferred_element_type=F32
    )
    carried = jnp.dot(
        jnp.concatenate([first[LEV:], second[LEV:]], axis=1), average, preferred_element_type=F32
    )
    moving = velocity * levels_mask
    flux = jnp.concatenate([carried[:LEV] * moving, carried[LEV:] * moving], axis=0).astype(BF16)
    change = (-slope - drag_rate * velocity) * levels_mask
    return flux, advance(anchor, velocity, change, keep_share)


def cell_step(block, fluxes_ref, sources_ref, first_block, own, whole, tiles_ref):
    picked = []
    for t in range(6):
        offset = sources_ref[t, block] - 3 * first_block
        offset = jnp.where(offset > 3 * own + 2, offset - 3 * whole, jnp.where(offset < -3, offset + 3 * whole, offset))
        picked.append(fluxes_ref[offset + 3])
    return -jnp.dot(jnp.concatenate(picked, axis=1), tiles_ref[block], preferred_element_type=F32)


def other_block(sources_ref, edge, first_block, own, whole):
    offset = sources_ref[1, edge] - first_block
    return jnp.where(offset > own, offset - whole, jnp.where(offset < -1, offset + whole, offset))


def start_kernel(
    own, thickness, tracer, velocity, levels, average, edge_sources, cell_sources,
    inner, outer, levels_out, edge_sources_out, cell_sources_out,
    h, s, v, flat, sems,
):
    position = lax.axis_index("dom")
    whole = own * lax.axis_size("dom")
    inner_side = 1 - lax.rem(position, 2)
    ends = []
    for p, side in ((0, inner_side), (1, 1 - inner_side)):
        block = side * (own - 1)
        ends.append((p, side, block, block + 1 - 2 * side))

    def columns(block, wide):
        return pl.ds(pl.multiple_of(block * TILE, TILE), wide)

    small = [
        pltpu.make_async_copy(levels, flat, sems.at[0]),
        pltpu.make_async_copy(edge_sources, edge_sources_out, sems.at[1]),
        pltpu.make_async_copy(cell_sources, cell_sources_out, sems.at[2]),
    ]
    fields, tiles = [], []
    for p, side, block, after in ends:
        for k, b in ((0, block), (1, after)):
            fields.append(pltpu.make_async_copy(thickness.at[:, columns(b, TILE)], h.at[p, k], sems.at[3 + 4 * p + 2 * k]))
            fields.append(pltpu.make_async_copy(tracer.at[:, columns(b, TILE)], s.at[p, k], sems.at[4 + 4 * p + 2 * k]))
        fields.append(pltpu.make_async_copy(velocity.at[:, columns(3 * block, 3 * TILE)], v.at[p], sems.at[11 + p]))
        message = (inner, outer)[p]
        rows = pl.ds(pl.multiple_of(block * 6 * TILE, 6 * TILE), 6 * TILE)
        tiles.append(pltpu.make_async_copy(average.at[rows, :], message.at[pl.ds(SIDE, 6 * TILE), :], sems.at[13 + p]))
    for copy in small + fields + tiles:
        copy.start()
    above = above_weights()
    for copy in small:
        copy.wait()
    for block in range(own):
        levels_out[block] = flat[lanes(block)]
    for copy in fields:
        copy.wait()
    done = []
    for p, side, block, after in ends:
        depth = lax.broadcasted_iota(jnp.int32, (LEV, TILE), 0)
        done.append((h[p, 0], s[p, 0], (depth < levels_out[pl.ds(block, 1), :]).astype(F32)))
    pressures = pressure_of(done, above)
    for p, side, block, after in ends:
        message = (inner, outer)[p]
        mask = done[p][2]
        message[0:LEV, :] = pressures[:, lanes(p)].astype(BF16)
        message[LEV : 2 * LEV, :] = h[p, 0].astype(BF16)
        message[2 * LEV : NEAR, :] = s[p, 0].astype(BF16)
        message[NEAR : NEAR + LEV, :] = h[p, 1].astype(BF16)
        message[NEAR + LEV : NEXT, :] = s[p, 1].astype(BF16)
        row = lax.broadcasted_iota(jnp.int32, (16, TILE), 0)
        signs = jnp.zeros((16, TILE), F32)
        for j in range(3):
            message[NEXT + j * LEV : NEXT + (j + 1) * LEV, :] = (v[p, :, lanes(j)] * mask).astype(BF16)
            low = other_block(edge_sources_out, j, position * own, own, whole)
            high = other_block(edge_sources_out, 3 * (own - 1) + j, position * own, own, whole) - (own - 1)
            signs = jnp.where(row == j, jnp.where(side == 0, low, high).astype(F32), signs)
        message[MOVE:SIDE, :] = signs.astype(BF16)
    for copy in tiles:
        copy.wait()


def first_inside(
    own, keep_share, h0, s0, v0, levels, gradient, average, edge_sources, divergence, cell_sources,
    fluxes, new_coded, new_thickness, new_tracer, new_velocity, coded,
):
    done = [(h0[:, lanes(b)], s0[:, lanes(b)], block_mask(levels, b)) for b in range(own)]
    code_blocks(coded, range(own), done, above_weights())
    inside_edges(own, keep_share, coded, v0, v0, levels, gradient, average, edge_sources, fluxes, new_velocity)
    inside_cells(
        own, keep_share, fluxes, h0, s0, h0, s0, levels, divergence, cell_sources,
        new_coded, new_thickness, new_tracer,
    )


def on(places, work):
    place = lax.rem(lax.axis_index("dom"), 8)
    here = place == places[0]
    for other in places[1:]:
        here = here | (place == other)
    pl.when(here)(work)


def inside(
    places, edge_blocks, cell_blocks,
    own, keep_share, coded, velocity, velocity0, levels, gradient, average, edge_sources,
    thickness, tracer, thickness0, tracer0, divergence, cell_sources, *refs,
):
    fluxes, new_velocity, new_thickness, new_tracer = refs[-4:]

    def work():
        inside_edges(
            own, keep_share, coded, velocity, velocity0, levels, gradient, average, edge_sources, fluxes, new_velocity,
            edge_blocks,
        )
        inside_cells(
            own, keep_share, fluxes, thickness, tracer, thickness0, tracer0, levels, divergence, cell_sources,
            None, new_thickness, new_tracer, cell_blocks,
        )

    on(places, work)


def whole_inside(
    own, keep_share, coded, velocity, velocity0, levels, gradient, average, edge_sources,
    thickness, tracer, thickness0, tracer0, divergence, cell_sources,
    fluxes, new_coded, new_thickness, new_tracer, new_velocity,
):
    inside_edges(
        own, keep_share, coded, velocity, velocity0, levels, gradient, average, edge_sources, fluxes, new_velocity
    )
    inside_cells(
        own, keep_share, fluxes, thickness, tracer, thickness0, tracer0, levels, divergence, cell_sources,
        new_coded, new_thickness, new_tracer,
    )


def tick(own, keep_share, *refs):
    pass


def inside_edges(
    own, keep_share, coded, velocity, velocity0, levels, gradient, average, edge_sources, fluxes, new_velocity,
    blocks=None,
):
    whole = own * lax.axis_size("dom")
    first_block = lax.axis_index("dom") * own
    for block in blocks or range(1, own - 1):
        mask = block_mask(levels, block)
        for edge in range(3 * block, 3 * block + 3):
            other = other_block(edge_sources, edge, first_block, own, whole)
            flux, updated = edge_step(
                mask, coded[block], coded[other], gradient[edge], average[edge],
                velocity[:, lanes(edge)], velocity0[:, lanes(edge)], keep_share,
            )
            fluxes[edge + 3] = flux
            new_velocity[:, lanes(edge)] = updated


def inside_cells(
    own, keep_share, fluxes, thickness, tracer, thickness0, tracer0, levels, divergence, cell_sources,
    new_coded, new_thickness, new_tracer, blocks=None,
):
    whole = own * lax.axis_size("dom")
    first_block = lax.axis_index("dom") * own
    done = []
    for block in blocks or range(2, own - 2):
        done.append(
            finish_cell(
                block, own, keep_share, first_block, whole,
                thickness, tracer, thickness0, tracer0, levels, divergence, cell_sources,
                fluxes, new_thickness, new_tracer,
            )
        )
    if new_coded is not None:
        code_blocks(new_coded, range(2, own - 2), done, above_weights())


def finish_cell(
    block, own, keep_share, first_block, whole,
    thickness, tracer, thickness0, tracer0, levels, divergence, cell_sources,
    fluxes, new_thickness, new_tracer,
):
    at = lanes(block)
    mask = block_mask(levels, block)
    change = cell_step(block, fluxes, cell_sources, first_block, own, whole, divergence)
    h = advance(thickness0[:, at], thickness[:, at], change[:LEV] * mask, keep_share)
    s = advance(tracer0[:, at], tracer[:, at], change[LEV:] * mask, keep_share)
    new_thickness[:, at] = h
    new_tracer[:, at] = s
    return h, s, mask


def rim_step(
    odd, own, keep_share, last,
    outer_in, inner_in, tiles_outer, tiles_inner,
    coded, thickness, tracer, velocity, thickness0, tracer0, velocity0, levels,
    gradient, average, edge_sources, divergence, cell_sources,
    fluxes, new_coded, new_thickness, new_tracer, new_velocity, pair,
    inner, outer, send,
):
    above = above_weights()
    first_block = lax.axis_index("dom") * own
    whole = own * lax.axis_size("dom")
    halos = (inner_in, outer_in) if odd else (outer_in, inner_in)
    halo_tiles = (tiles_inner, tiles_outer) if odd else (tiles_outer, tiles_inner)
    messages = (inner, outer) if odd else (outer, inner)
    ends = ((0, 0, 1), (1, own - 1, own - 2))

    for side, block, after in ends:
        mask = block_mask(levels, block)
        outward = 2 * side - 1
        beyond = -1 if side == 0 else own
        halo, tiles = halos[side], halo_tiles[side]
        pair[side, 0] = halo[0:NEAR, :]
        pair[side, 1] = coded[after]
        signs = tiles[MOVE:SIDE, :].astype(F32)
        for j in range(3):
            edge = 3 * block + j
            other = other_block(edge_sources, edge, first_block, own, whole)
            flux, updated = edge_step(
                mask, coded[block], pair[side, (other == after).astype(jnp.int32)], gradient[edge], average[edge],
                velocity[:, lanes(edge)], velocity0[:, lanes(edge)], keep_share,
            )
            fluxes[edge + 3] = flux
            new_velocity[:, lanes(edge)] = updated
            toward = signs[j : j + 1, :] * outward
            second = jnp.where(
                jnp.broadcast_to(toward, (2 * LEV, TILE)) > 0.0,
                halo[NEAR:NEXT, :].astype(F32),
                coded[block, LEV:, :].astype(F32),
            ).astype(BF16)
            carried = jnp.dot(
                jnp.concatenate([halo[LEV:NEAR, :], second], axis=1),
                tiles[SIDE + j * 256 : SIDE + (j + 1) * 256, :],
                preferred_element_type=F32,
            )
            moving = halo[NEXT + j * LEV : NEXT + (j + 1) * LEV, :].astype(F32)
            fluxes[3 * beyond + 3 + j] = jnp.concatenate(
                [carried[:LEV] * moving, carried[LEV:] * moving], axis=0
            ).astype(BF16)
            if not last:
                messages[side][NEXT + j * LEV : NEXT + (j + 1) * LEV, :] = (updated * mask).astype(BF16)
        if last:
            send(2, 3 * block, 3)
    rim = (0, 1, own - 2, own - 1)
    done = []
    for block in rim:
        done.append(
            finish_cell(
                block, own, keep_share, first_block, whole,
                thickness, tracer, thickness0, tracer0, levels, divergence, cell_sources,
                fluxes, new_thickness, new_tracer,
            )
        )
        if last and block in (1, own - 1):
            send(0, block - 1, 2)
            send(1, block - 1, 2)
    if last:
        return
    code_blocks(new_coded, rim, done, above)
    for side, block, after in ends:
        messages[side][0:NEAR, :] = new_coded[block]
        messages[side][NEAR:NEXT, :] = new_coded[after, LEV:, :]


def rim_kernel(odd, second, own, keep_share, *refs):
    common = refs[:17]
    out = refs[17 + 5 + (1 if second else 0) :]
    built, inner, outer, pair = out[:5], out[5], out[6], out[7]

    @pl.when(lax.rem(lax.axis_index("dom"), 2) == (1 if odd else 0))
    def _():
        rim_step(odd, own, keep_share, False, *common, *built, pair, inner, outer, None)


def last_rim_kernel(own, keep_share, *refs):
    inner_in, up_in, down_in, tiles_inner, tiles_up, tiles_down = refs[:6]
    common = refs[6:19]
    fluxes, h, s, v, far_h, far_s, far_v, pair, sems = refs[23:]
    here, far = (h, s, v), (far_h, far_s, far_v)
    odd_here = lax.rem(lax.axis_index("dom"), 2)
    whole = []
    for which in (2, 0, 1):
        lo, wide = (3, 3 * (own - 2)) if which == 2 else (2, own - 4)
        at = (slice(None), pl.ds(lo * TILE, wide * TILE))
        whole.append(pltpu.make_async_copy(here[which].at[at], far[which].at[at], sems.at[which]))
        whole[-1].start()

    for odd in (False, True):

        @pl.when(odd_here == (1 if odd else 0))
        def _(odd=odd):
            sent = []

            def send(which, lo, wide):
                at = (slice(None), pl.ds(lo * TILE, wide * TILE))
                copy = pltpu.make_async_copy(here[which].at[at], far[which].at[at], sems.at[3 + len(sent)])
                copy.start()
                sent.append(copy)

            rim_step(
                odd, own, keep_share, True,
                down_in if odd else up_in, inner_in, tiles_down if odd else tiles_up, tiles_inner,
                *common, fluxes, None, h, s, v, pair, None, None, send,
            )
            for copy in sent:
                copy.wait()

    for copy in whole:
        copy.wait()


def in_vmem(array):
    return pltpu.with_memory_space_constraint(array, pltpu.VMEM)


def in_hbm(array):
    return pltpu.with_memory_space_constraint(array, pltpu.HBM)


def local(
    thickness,
    tracer,
    velocity,
    active_levels,
    gradient_tiles,
    average_tiles,
    edge_sources,
    divergence_tiles,
    cell_sources,
):
    own = cell_sources.shape[0]
    devices = lax.axis_size("dom")
    within = [(i, i ^ 1) for i in range(devices)]
    upward = [(i, (i + 1) % devices) for i in range(devices)]
    filler = {1: 1, 3: -3, 5: -1, 7: -1}
    downward = [(i, (i + filler[i % 8]) % devices if i % 2 else (i - 1) % devices) for i in range(devices)]
    cells, edges = thickness.shape[1], velocity.shape[1]
    vmem = pl.BlockSpec(memory_space=pltpu.VMEM)
    hbm = pl.BlockSpec(memory_space=pltpu.HBM)
    params = pltpu.CompilerParams(vmem_limit_bytes=16 * 1024 * 1024)

    gradient = (gradient_tiles.reshape(3 * own, 2 * TILE, TILE))
    average = (average_tiles.reshape(3 * own, 2 * TILE, TILE))
    average_rows = in_hbm(average_tiles.reshape(3 * own * 2 * TILE, TILE))
    divergence = (divergence_tiles.reshape(own, 6 * TILE, TILE))
    first_rows = SIDE + 6 * TILE

    def message(rows):
        return pltpu.VMEM((rows, TILE), BF16)

    inner, outer, levels, edge_sources, cell_sources = pl.pallas_call(
        lambda *refs: start_kernel(own, *refs),
        out_shape=(
            message(first_rows),
            message(first_rows),
            pltpu.VMEM((own, TILE), jnp.int32),
            pltpu.VMEM((2, 3 * own), jnp.int32),
            pltpu.VMEM((6, own), jnp.int32),
        ),
        in_specs=[hbm] * 7,
        out_specs=[vmem] * 5,
        scratch_shapes=[
            pltpu.VMEM((2, 2, LEV, TILE), F32),
            pltpu.VMEM((2, 2, LEV, TILE), F32),
            pltpu.VMEM((2, LEV, 3 * TILE), F32),
            pltpu.VMEM((cells,), jnp.int32),
            pltpu.SemaphoreType.DMA((15,)),
        ],
        compiler_params=params,
        cost_estimate=pl.CostEstimate(flops=2 * 10**10, bytes_accessed=10**6, transcendentals=0),
        name="start",
    )(in_hbm(thickness), in_hbm(tracer), in_hbm(velocity), in_hbm(active_levels), average_rows, in_hbm(edge_sources.T), in_hbm(cell_sources.T))

    coded_shape = pltpu.VMEM((own, NEAR, TILE), BF16)
    field_shapes = (
        pltpu.VMEM((LEV, cells), F32),
        pltpu.VMEM((LEV, cells), F32),
        pltpu.VMEM((LEV, edges), F32),
    )
    flux_shape = pltpu.VMEM((3 * own + 6, 2 * LEV, TILE), BF16)
    built_shapes = (flux_shape, coded_shape) + field_shapes
    pair_scratch = pltpu.VMEM((2, 2, NEAR, TILE), BF16)

    def send_up(x):
        return lax.ppermute(x, "dom", upward)

    def send_down(x):
        return lax.ppermute(x, "dom", downward)

    def swap_inner(x):
        return lax.ppermute(x, "dom", within)

    def rim(odd, keep_share, inner_in, outer_in, tiles_outer, common, built, inner):
        second = inner is not None
        extra = (inner,) if second else ()
        out = pl.pallas_call(
            lambda *refs: rim_kernel(odd, second, own, keep_share, *refs),
            out_shape=built_shapes + (message(MOVE), message(MOVE)),
            in_specs=[vmem] * (17 + 5 + len(extra)),
            out_specs=[vmem] * 7,
            scratch_shapes=[pair_scratch],
            input_output_aliases={17 + i: i for i in range(5 + len(extra))},
            compiler_params=params,
            cost_estimate=LARGE,
            name="rim_odd" if odd else "rim_even",
        )(outer_in, inner_in, tiles_outer, tiles_inner, *common, *built, *extra)
        return out[:5], out[5], out[6]

    def call(body, keep_share, operands, shapes, specs, scratch, name, after=None, passed=None, filled=()):
        n = len(operands)
        extra = tuple(x for x in (after, passed) if x is not None)
        given = tuple(x for x in (passed,) if x is not None) + filled
        total = n + len(extra) + len(filled)
        first = 0 if passed is None else 1
        return pl.pallas_call(
            lambda *refs: body(own, keep_share, *refs[:n], *refs[n + len(extra) : total], *refs[total + first :]),
            out_shape=tuple(pltpu.VMEM(x.shape, x.dtype) for x in given) + shapes,
            in_specs=[vmem] * total,
            out_specs=[vmem] * len(given) + specs,
            input_output_aliases={total - len(given) + i: i for i in range(len(given))},
            scratch_shapes=scratch,
            compiler_params=params,
            cost_estimate=SMALL,
            name=name,
        )(*operands, *extra, *filled)

    up_in, down_in = lax.ppermute(outer, "dom", upward), lax.ppermute(outer, "dom", [(j, i) for i, j in upward])
    anchor = (in_vmem(thickness), in_vmem(tracer), in_vmem(velocity))
    gradient, average, divergence = in_vmem(gradient), in_vmem(average), in_vmem(divergence)
    loaded = call(
        first_inside, keep_shares[0],
        (*anchor, levels, gradient, average, edge_sources, divergence, cell_sources),
        built_shapes + (coded_shape,), [vmem] * 6, [], "inside",
    )
    built, coded = loaded[:5], loaded[5]
    inner_in = swap_inner(inner)
    tiles_up, tiles_down, tiles_inner = up_in, down_in, inner_in

    def operands(coded, state):
        return (coded, *state, *anchor, levels, gradient, average, edge_sources, divergence, cell_sources)

    common = operands(coded, anchor)
    built, inner, outer = rim(False, keep_shares[0], inner_in, up_in, tiles_up, common, built, None)
    next_down = send_down(outer)
    built, inner, outer = rim(True, keep_shares[0], inner_in, down_in, tiles_down, common, built, inner)
    next_up = send_up(outer)
    up_in, down_in, inner_in = next_up, next_down, swap_inner(inner)

    def inside_operands(coded, thickness, tracer, velocity):
        return (
            coded, velocity, anchor[2], levels, gradient, average, edge_sources,
            thickness, tracer, anchor[0], anchor[1], divergence, cell_sources,
        )

    common = operands(built[1], built[2:5])
    built = call(
        whole_inside, keep_shares[1], inside_operands(*common[:4]), built_shapes, [vmem] * 5, [], "inside"
    )
    fluxes = call(tick, 0.0, (down_in,), (), [], [], "tick", passed=built[0])[0]
    built = (fluxes, *built[1:])
    built, inner, outer = rim(True, keep_shares[1], inner_in, down_in, tiles_down, common, built, None)
    next_up = send_up(outer)
    middle, near_middle = range(3, own - 3), range(4, own - 4)
    inner, fluxes, new_velocity, h, s = call(
        functools.partial(inside, EVEN, middle, near_middle), keep_shares[2], inside_operands(*built[1:]),
        (flux_shape, field_shapes[2]) + field_shapes[:2], [vmem] * 4, [], "even_middle", passed=inner,
    )
    built, inner, outer = rim(False, keep_shares[1], inner_in, up_in, tiles_up, common, built, inner)

    common = operands(built[1], built[2:5])
    outer, fluxes, new_velocity, h, s = call(
        functools.partial(inside, (3,), None, None), keep_shares[2], inside_operands(*common[:4]),
        (), [], [], "odd_inside", passed=outer, filled=(fluxes, new_velocity, h, s),
    )
    up_in, down_in = next_up, send_down(outer)

    far_shapes = (pltpu.HBM((LEV, cells), F32), pltpu.HBM((LEV, cells), F32), pltpu.HBM((LEV, edges), F32))
    inner, fluxes, new_velocity, h, s = call(
        functools.partial(inside, (1, 5, 7), None, None), keep_shares[2], inside_operands(*common[:4]),
        (), [], [], "odd_inside", passed=inner, filled=(fluxes, new_velocity, h, s),
    )
    inner_in = swap_inner(inner)
    fluxes = call(tick, 0.0, (up_in,), (), [], [], "tick", passed=fluxes)[0]
    edge_rest = [b for b in range(1, own - 1) if b not in middle]
    cell_rest = [b for b in range(2, own - 2) if b not in near_middle]
    fluxes, new_velocity, h, s = call(
        functools.partial(inside, EVEN, edge_rest, cell_rest), keep_shares[2], inside_operands(*common[:4]),
        (), [], [], "even_rest", filled=(fluxes, new_velocity, h, s),
    )
    h = call(tick, 0.0, (down_in,), (), [], [], "tick", passed=h)[0]
    results = pl.pallas_call(
        lambda *refs: last_rim_kernel(own, keep_shares[2], *refs),
        out_shape=(flux_shape,) + field_shapes + far_shapes,
        in_specs=[vmem] * 23,
        out_specs=[vmem] * 4 + [hbm] * 3,
        scratch_shapes=[pair_scratch, pltpu.SemaphoreType.DMA((9,))],
        input_output_aliases={19 + i: i for i in range(4)},
        compiler_params=params,
        cost_estimate=SMALL,
        name="rim",
    )(inner_in, up_in, down_in, tiles_inner, tiles_up, tiles_down, *common, fluxes, h, s, new_velocity)
    return results[4:]


def solution(mesh):
    return jax.shard_map(
        local,
        mesh=mesh,
        in_specs=(
            P(None, "dom"),
            P(None, "dom"),
            P(None, "dom"),
            P("dom"),
            P("dom", None, None, None),
            P("dom", None, None, None),
            P("dom", None),
            P("dom", None, None, None),
            P("dom", None),
        ),
        out_specs=(P(None, "dom"), P(None, "dom"), P(None, "dom")),
        check_vma=False,
    )
```

```python
import functools

import jax
import jax.numpy as jnp
from jax import lax
from jax.experimental import pallas as pl
from jax.experimental.pallas import tpu as pltpu
from jax.sharding import PartitionSpec as P

buoyancy = 0.2
drag_rate = 0.5
time_step = 0.25
keep_shares = (0.0, 0.75, 1.0 / 3.0)

F32 = jnp.float32
BF16 = jnp.bfloat16
LEV = 80
EVEN = (0, 2, 4, 6)
TILE = 128
SMALL = pl.CostEstimate(flops=1000, bytes_accessed=1000, transcendentals=0)
FIRST = pl.CostEstimate(flops=10**10, bytes_accessed=10**7, transcendentals=0)
LARGE = pl.CostEstimate(flops=10**9, bytes_accessed=10**6, transcendentals=0)
NEAR = 3 * LEV
NEXT = NEAR + 2 * LEV
MOVE = NEXT + 3 * LEV
SIDE = MOVE + 16


def lanes(block):
    return slice(block * TILE, (block + 1) * TILE)


def advance(anchor, current, slope, keep_share):
    if keep_share == 0.0:
        return current + time_step * slope
    return keep_share * anchor + (1.0 - keep_share) * (current + time_step * slope)


def block_mask(levels_ref, block):
    depth = lax.broadcasted_iota(jnp.int32, (LEV, TILE), 0)
    return (depth < levels_ref[block : block + 1, :]).astype(F32)


def above_weights():
    row = lax.broadcasted_iota(jnp.int32, (LEV, 3 * LEV), 0)
    column = lax.broadcasted_iota(jnp.int32, (LEV, 3 * LEV), 1)
    column = jnp.where(column >= 2 * LEV, column - 2 * LEV, jnp.where(column >= LEV, column - LEV, column))
    return jnp.where(column < row, 1.0, jnp.where(column == row, 0.5, 0.0)).astype(BF16)


def pressure_of(done, above):
    highs, middles, lows = [], [], []
    for thickness, tracer, mask in done:
        weight = thickness * (1.0 - buoyancy * tracer) * mask
        high = weight.astype(BF16)
        rest = weight - high.astype(F32)
        middle = rest.astype(BF16)
        highs.append(high)
        middles.append(middle)
        lows.append((rest - middle.astype(F32)).astype(BF16))
    parts = jnp.concatenate([jnp.concatenate(p, axis=1) for p in (highs, middles, lows)], axis=0)
    return jnp.dot(above, parts, preferred_element_type=F32) * (1.0 / LEV)


def code_blocks(coded, blocks, done, above):
    pressures = pressure_of(done, above)
    for i, (block, (thickness, tracer, mask)) in enumerate(zip(blocks, done)):
        coded[block, 0:LEV, :] = pressures[:, lanes(i)].astype(BF16)
        coded[block, LEV : 2 * LEV, :] = thickness.astype(BF16)
        coded[block, 2 * LEV : NEAR, :] = tracer.astype(BF16)


def edge_step(levels_mask, first, second, gradient, average, velocity, anchor, keep_share):
    slope = jnp.dot(
        jnp.concatenate([first[:LEV], second[:LEV]], axis=1), gradient, preferred_element_type=F32
    )
    carried = jnp.dot(
        jnp.concatenate([first[LEV:], second[LEV:]], axis=1), average, preferred_element_type=F32
    )
    moving = velocity * levels_mask
    flux = jnp.concatenate([carried[:LEV] * moving, carried[LEV:] * moving], axis=0).astype(BF16)
    change = (-slope - drag_rate * velocity) * levels_mask
    return flux, advance(anchor, velocity, change, keep_share)


def cell_step(block, fluxes_ref, sources_ref, first_block, own, whole, tiles_ref):
    picked = []
    for t in range(6):
        offset = sources_ref[t, block] - 3 * first_block
        offset = jnp.where(offset > 3 * own + 2, offset - 3 * whole, jnp.where(offset < -3, offset + 3 * whole, offset))
        picked.append(fluxes_ref[offset + 3])
    return -jnp.dot(jnp.concatenate(picked, axis=1), tiles_ref[block], preferred_element_type=F32)


def other_block(sources_ref, edge, first_block, own, whole):
    offset = sources_ref[1, edge] - first_block
    return jnp.where(offset > own, offset - whole, jnp.where(offset < -1, offset + whole, offset))


def start_kernel(
    own, thickness, tracer, velocity, levels, average, edge_sources, cell_sources,
    inner, outer, levels_out, edge_sources_out, cell_sources_out,
    h, s, v, flat, sems,
):
    position = lax.axis_index("dom")
    whole = own * lax.axis_size("dom")
    inner_side = 1 - lax.rem(position, 2)
    ends = []
    for p, side in ((0, inner_side), (1, 1 - inner_side)):
        block = side * (own - 1)
        ends.append((p, side, block, block + 1 - 2 * side))

    def columns(block, wide):
        return pl.ds(pl.multiple_of(block * TILE, TILE), wide)

    small = [
        pltpu.make_async_copy(levels, flat, sems.at[0]),
        pltpu.make_async_copy(edge_sources, edge_sources_out, sems.at[1]),
        pltpu.make_async_copy(cell_sources, cell_sources_out, sems.at[2]),
    ]
    fields, tiles = [], []
    for p, side, block, after in ends:
        for k, b in ((0, block), (1, after)):
            fields.append(pltpu.make_async_copy(thickness.at[:, columns(b, TILE)], h.at[p, k], sems.at[3 + 4 * p + 2 * k]))
            fields.append(pltpu.make_async_copy(tracer.at[:, columns(b, TILE)], s.at[p, k], sems.at[4 + 4 * p + 2 * k]))
        fields.append(pltpu.make_async_copy(velocity.at[:, columns(3 * block, 3 * TILE)], v.at[p], sems.at[11 + p]))
        message = (inner, outer)[p]
        rows = pl.ds(pl.multiple_of(block * 6 * TILE, 6 * TILE), 6 * TILE)
        tiles.append(pltpu.make_async_copy(average.at[rows, :], message.at[pl.ds(SIDE, 6 * TILE), :], sems.at[13 + p]))
    for copy in small + fields + tiles:
        copy.start()
    above = above_weights()
    for copy in small:
        copy.wait()
    for block in range(own):
        levels_out[block] = flat[lanes(block)]
    for copy in fields:
        copy.wait()
    done = []
    for p, side, block, after in ends:
        depth = lax.broadcasted_iota(jnp.int32, (LEV, TILE), 0)
        done.append((h[p, 0], s[p, 0], (depth < levels_out[pl.ds(block, 1), :]).astype(F32)))
    pressures = pressure_of(done, above)
    for p, side, block, after in ends:
        message = (inner, outer)[p]
        mask = done[p][2]
        message[0:LEV, :] = pressures[:, lanes(p)].astype(BF16)
        message[LEV : 2 * LEV, :] = h[p, 0].astype(BF16)
        message[2 * LEV : NEAR, :] = s[p, 0].astype(BF16)
        message[NEAR : NEAR + LEV, :] = h[p, 1].astype(BF16)
        message[NEAR + LEV : NEXT, :] = s[p, 1].astype(BF16)
        row = lax.broadcasted_iota(jnp.int32, (16, TILE), 0)
        signs = jnp.zeros((16, TILE), F32)
        for j in range(3):
            message[NEXT + j * LEV : NEXT + (j + 1) * LEV, :] = (v[p, :, lanes(j)] * mask).astype(BF16)
            low = other_block(edge_sources_out, j, position * own, own, whole)
            high = other_block(edge_sources_out, 3 * (own - 1) + j, position * own, own, whole) - (own - 1)
            signs = jnp.where(row == j, jnp.where(side == 0, low, high).astype(F32), signs)
        message[MOVE:SIDE, :] = signs.astype(BF16)
    for copy in tiles:
        copy.wait()


def first_inside(
    own, keep_share, h0, s0, v0, levels, gradient, average, edge_sources, divergence, cell_sources,
    fluxes, new_coded, new_thickness, new_tracer, new_velocity, coded,
):
    done = [(h0[:, lanes(b)], s0[:, lanes(b)], block_mask(levels, b)) for b in range(own)]
    code_blocks(coded, range(own), done, above_weights())
    inside_edges(own, keep_share, coded, v0, v0, levels, gradient, average, edge_sources, fluxes, new_velocity)
    inside_cells(
        own, keep_share, fluxes, h0, s0, h0, s0, levels, divergence, cell_sources,
        new_coded, new_thickness, new_tracer,
    )


def on(places, work):
    place = lax.rem(lax.axis_index("dom"), 8)
    here = place == places[0]
    for other in places[1:]:
        here = here | (place == other)
    pl.when(here)(work)


def inside(
    places, edge_blocks, cell_blocks,
    own, keep_share, coded, velocity, velocity0, levels, gradient, average, edge_sources,
    thickness, tracer, thickness0, tracer0, divergence, cell_sources, *refs,
):
    fluxes, new_velocity, new_thickness, new_tracer = refs[-4:]

    def work():
        inside_edges(
            own, keep_share, coded, velocity, velocity0, levels, gradient, average, edge_sources, fluxes, new_velocity,
            edge_blocks,
        )
        inside_cells(
            own, keep_share, fluxes, thickness, tracer, thickness0, tracer0, levels, divergence, cell_sources,
            None, new_thickness, new_tracer, cell_blocks,
        )

    on(places, work)


def whole_inside(
    own, keep_share, coded, velocity, velocity0, levels, gradient, average, edge_sources,
    thickness, tracer, thickness0, tracer0, divergence, cell_sources,
    fluxes, new_coded, new_thickness, new_tracer, new_velocity,
):
    inside_edges(
        own, keep_share, coded, velocity, velocity0, levels, gradient, average, edge_sources, fluxes, new_velocity
    )
    inside_cells(
        own, keep_share, fluxes, thickness, tracer, thickness0, tracer0, levels, divergence, cell_sources,
        new_coded, new_thickness, new_tracer,
    )


def tick(own, keep_share, *refs):
    pass


def inside_edges(
    own, keep_share, coded, velocity, velocity0, levels, gradient, average, edge_sources, fluxes, new_velocity,
    blocks=None,
):
    whole = own * lax.axis_size("dom")
    first_block = lax.axis_index("dom") * own
    for block in blocks or range(1, own - 1):
        mask = block_mask(levels, block)
        for edge in range(3 * block, 3 * block + 3):
            other = other_block(edge_sources, edge, first_block, own, whole)
            flux, updated = edge_step(
                mask, coded[block], coded[other], gradient[edge], average[edge],
                velocity[:, lanes(edge)], velocity0[:, lanes(edge)], keep_share,
            )
            fluxes[edge + 3] = flux
            new_velocity[:, lanes(edge)] = updated


def inside_cells(
    own, keep_share, fluxes, thickness, tracer, thickness0, tracer0, levels, divergence, cell_sources,
    new_coded, new_thickness, new_tracer, blocks=None,
):
    whole = own * lax.axis_size("dom")
    first_block = lax.axis_index("dom") * own
    done = []
    for block in blocks or range(2, own - 2):
        done.append(
            finish_cell(
                block, own, keep_share, first_block, whole,
                thickness, tracer, thickness0, tracer0, levels, divergence, cell_sources,
                fluxes, new_thickness, new_tracer,
            )
        )
    if new_coded is not None:
        code_blocks(new_coded, range(2, own - 2), done, above_weights())


def finish_cell(
    block, own, keep_share, first_block, whole,
    thickness, tracer, thickness0, tracer0, levels, divergence, cell_sources,
    fluxes, new_thickness, new_tracer,
):
    at = lanes(block)
    mask = block_mask(levels, block)
    change = cell_step(block, fluxes, cell_sources, first_block, own, whole, divergence)
    h = advance(thickness0[:, at], thickness[:, at], change[:LEV] * mask, keep_share)
    s = advance(tracer0[:, at], tracer[:, at], change[LEV:] * mask, keep_share)
    new_thickness[:, at] = h
    new_tracer[:, at] = s
    return h, s, mask


def rim_step(
    odd, own, keep_share, last,
    outer_in, inner_in, tiles_outer, tiles_inner,
    coded, thickness, tracer, velocity, thickness0, tracer0, velocity0, levels,
    gradient, average, edge_sources, divergence, cell_sources,
    fluxes, new_coded, new_thickness, new_tracer, new_velocity, pair,
    inner, outer, send,
):
    above = above_weights()
    first_block = lax.axis_index("dom") * own
    whole = own * lax.axis_size("dom")
    halos = (inner_in, outer_in) if odd else (outer_in, inner_in)
    halo_tiles = (tiles_inner, tiles_outer) if odd else (tiles_outer, tiles_inner)
    messages = (inner, outer) if odd else (outer, inner)
    ends = ((0, 0, 1), (1, own - 1, own - 2))

    for side, block, after in ends:
        mask = block_mask(levels, block)
        outward = 2 * side - 1
        beyond = -1 if side == 0 else own
        halo, tiles = halos[side], halo_tiles[side]
        pair[side, 0] = halo[0:NEAR, :]
        pair[side, 1] = coded[after]
        signs = tiles[MOVE:SIDE, :].astype(F32)
        for j in range(3):
            edge = 3 * block + j
            other = other_block(edge_sources, edge, first_block, own, whole)
            flux, updated = edge_step(
                mask, coded[block], pair[side, (other == after).astype(jnp.int32)], gradient[edge], average[edge],
                velocity[:, lanes(edge)], velocity0[:, lanes(edge)], keep_share,
            )
            fluxes[edge + 3] = flux
            new_velocity[:, lanes(edge)] = updated
            toward = signs[j : j + 1, :] * outward
            second = jnp.where(
                jnp.broadcast_to(toward, (2 * LEV, TILE)) > 0.0,
                halo[NEAR:NEXT, :].astype(F32),
                coded[block, LEV:, :].astype(F32),
            ).astype(BF16)
            carried = jnp.dot(
                jnp.concatenate([halo[LEV:NEAR, :], second], axis=1),
                tiles[SIDE + j * 256 : SIDE + (j + 1) * 256, :],
                preferred_element_type=F32,
            )
            moving = halo[NEXT + j * LEV : NEXT + (j + 1) * LEV, :].astype(F32)
            fluxes[3 * beyond + 3 + j] = jnp.concatenate(
                [carried[:LEV] * moving, carried[LEV:] * moving], axis=0
            ).astype(BF16)
            if not last:
                messages[side][NEXT + j * LEV : NEXT + (j + 1) * LEV, :] = (updated * mask).astype(BF16)
        if last:
            send(2, 3 * block, 3)
    rim = (0, 1, own - 2, own - 1)
    done = []
    for block in rim:
        done.append(
            finish_cell(
                block, own, keep_share, first_block, whole,
                thickness, tracer, thickness0, tracer0, levels, divergence, cell_sources,
                fluxes, new_thickness, new_tracer,
            )
        )
        if last and block in (1, own - 1):
            send(0, block - 1, 2)
            send(1, block - 1, 2)
    if last:
        return
    code_blocks(new_coded, rim, done, above)
    for side, block, after in ends:
        messages[side][0:NEAR, :] = new_coded[block]
        messages[side][NEAR:NEXT, :] = new_coded[after, LEV:, :]


def rim_kernel(odd, second, own, keep_share, *refs):
    common = refs[:17]
    out = refs[17 + 5 + (1 if second else 0) :]
    built, inner, outer, pair = out[:5], out[5], out[6], out[7]

    @pl.when(lax.rem(lax.axis_index("dom"), 2) == (1 if odd else 0))
    def _():
        rim_step(odd, own, keep_share, False, *common, *built, pair, inner, outer, None)


def last_rim_kernel(own, keep_share, *refs):
    inner_in, up_in, down_in, tiles_inner, tiles_up, tiles_down = refs[:6]
    common = refs[6:19]
    fluxes, h, s, v, far_h, far_s, far_v, pair, sems = refs[23:]
    here, far = (h, s, v), (far_h, far_s, far_v)
    odd_here = lax.rem(lax.axis_index("dom"), 2)
    whole = []
    for which in (2, 0, 1):
        lo, wide = (3, 3 * (own - 2)) if which == 2 else (2, own - 4)
        at = (slice(None), pl.ds(lo * TILE, wide * TILE))
        whole.append(pltpu.make_async_copy(here[which].at[at], far[which].at[at], sems.at[which]))
        whole[-1].start()

    for odd in (False, True):

        @pl.when(odd_here == (1 if odd else 0))
        def _(odd=odd):
            sent = []

            def send(which, lo, wide):
                at = (slice(None), pl.ds(lo * TILE, wide * TILE))
                copy = pltpu.make_async_copy(here[which].at[at], far[which].at[at], sems.at[3 + len(sent)])
                copy.start()
                sent.append(copy)

            rim_step(
                odd, own, keep_share, True,
                down_in if odd else up_in, inner_in, tiles_down if odd else tiles_up, tiles_inner,
                *common, fluxes, None, h, s, v, pair, None, None, send,
            )
            for copy in sent:
                copy.wait()

    for copy in whole:
        copy.wait()


def in_vmem(array):
    return pltpu.with_memory_space_constraint(array, pltpu.VMEM)


def in_hbm(array):
    return pltpu.with_memory_space_constraint(array, pltpu.HBM)


def local(
    thickness,
    tracer,
    velocity,
    active_levels,
    gradient_tiles,
    average_tiles,
    edge_sources,
    divergence_tiles,
    cell_sources,
):
    own = cell_sources.shape[0]
    devices = lax.axis_size("dom")
    within = [(i, i ^ 1) for i in range(devices)]
    upward = [(i, (i + 1) % devices) for i in range(devices)]
    filler = {1: 1, 3: -3, 5: -1, 7: -1}
    downward = [(i, (i + filler[i % 8]) % devices if i % 2 else (i - 1) % devices) for i in range(devices)]
    cells, edges = thickness.shape[1], velocity.shape[1]
    vmem = pl.BlockSpec(memory_space=pltpu.VMEM)
    hbm = pl.BlockSpec(memory_space=pltpu.HBM)
    params = pltpu.CompilerParams(vmem_limit_bytes=16 * 1024 * 1024)

    gradient = (gradient_tiles.reshape(3 * own, 2 * TILE, TILE))
    average = (average_tiles.reshape(3 * own, 2 * TILE, TILE))
    average_rows = in_hbm(average_tiles.reshape(3 * own * 2 * TILE, TILE))
    divergence = (divergence_tiles.reshape(own, 6 * TILE, TILE))
    first_rows = SIDE + 6 * TILE

    def message(rows):
        return pltpu.VMEM((rows, TILE), BF16)

    inner, outer, levels, edge_sources, cell_sources = pl.pallas_call(
        lambda *refs: start_kernel(own, *refs),
        out_shape=(
            message(first_rows),
            message(first_rows),
            pltpu.VMEM((own, TILE), jnp.int32),
            pltpu.VMEM((2, 3 * own), jnp.int32),
            pltpu.VMEM((6, own), jnp.int32),
        ),
        in_specs=[hbm] * 7,
        out_specs=[vmem] * 5,
        scratch_shapes=[
            pltpu.VMEM((2, 2, LEV, TILE), F32),
            pltpu.VMEM((2, 2, LEV, TILE), F32),
            pltpu.VMEM((2, LEV, 3 * TILE), F32),
            pltpu.VMEM((cells,), jnp.int32),
            pltpu.SemaphoreType.DMA((15,)),
        ],
        compiler_params=params,
        cost_estimate=pl.CostEstimate(flops=2 * 10**10, bytes_accessed=10**6, transcendentals=0),
        name="start",
    )(in_hbm(thickness), in_hbm(tracer), in_hbm(velocity), in_hbm(active_levels), average_rows, in_hbm(edge_sources.T), in_hbm(cell_sources.T))

    coded_shape = pltpu.VMEM((own, NEAR, TILE), BF16)
    field_shapes = (
        pltpu.VMEM((LEV, cells), F32),
        pltpu.VMEM((LEV, cells), F32),
        pltpu.VMEM((LEV, edges), F32),
    )
    flux_shape = pltpu.VMEM((3 * own + 6, 2 * LEV, TILE), BF16)
    built_shapes = (flux_shape, coded_shape) + field_shapes
    pair_scratch = pltpu.VMEM((2, 2, NEAR, TILE), BF16)

    def send_up(x):
        return lax.ppermute(x, "dom", upward)

    def send_down(x):
        return lax.ppermute(x, "dom", downward)

    def swap_inner(x):
        return lax.ppermute(x, "dom", within)

    def rim(odd, keep_share, inner_in, outer_in, tiles_outer, common, built, inner):
        second = inner is not None
        extra = (inner,) if second else ()
        out = pl.pallas_call(
            lambda *refs: rim_kernel(odd, second, own, keep_share, *refs),
            out_shape=built_shapes + (message(MOVE), message(MOVE)),
            in_specs=[vmem] * (17 + 5 + len(extra)),
            out_specs=[vmem] * 7,
            scratch_shapes=[pair_scratch],
            input_output_aliases={17 + i: i for i in range(5 + len(extra))},
            compiler_params=params,
            cost_estimate=LARGE,
            name="rim_odd" if odd else "rim_even",
        )(outer_in, inner_in, tiles_outer, tiles_inner, *common, *built, *extra)
        return out[:5], out[5], out[6]

    def call(body, keep_share, operands, shapes, specs, scratch, name, after=None, passed=None, filled=()):
        n = len(operands)
        extra = tuple(x for x in (after, passed) if x is not None)
        given = tuple(x for x in (passed,) if x is not None) + filled
        total = n + len(extra) + len(filled)
        first = 0 if passed is None else 1
        return pl.pallas_call(
            lambda *refs: body(own, keep_share, *refs[:n], *refs[n + len(extra) : total], *refs[total + first :]),
            out_shape=tuple(pltpu.VMEM(x.shape, x.dtype) for x in given) + shapes,
            in_specs=[vmem] * total,
            out_specs=[vmem] * len(given) + specs,
            input_output_aliases={total - len(given) + i: i for i in range(len(given))},
            scratch_shapes=scratch,
            compiler_params=params,
            cost_estimate=FIRST if name == "first_inside" else SMALL,
            name=name,
        )(*operands, *extra, *filled)

    up_in, down_in = lax.ppermute(outer, "dom", upward), lax.ppermute(outer, "dom", [(j, i) for i, j in upward])
    anchor = (in_vmem(thickness), in_vmem(tracer), in_vmem(velocity))
    gradient, average, divergence = in_vmem(gradient), in_vmem(average), in_vmem(divergence)
    loaded = call(
        first_inside, keep_shares[0],
        (*anchor, levels, gradient, average, edge_sources, divergence, cell_sources),
        built_shapes + (coded_shape,), [vmem] * 6, [], "first_inside",
    )
    built, coded = loaded[:5], loaded[5]
    inner_in = swap_inner(inner)
    tiles_up, tiles_down, tiles_inner = up_in, down_in, inner_in

    def operands(coded, state):
        return (coded, *state, *anchor, levels, gradient, average, edge_sources, divergence, cell_sources)

    common = operands(coded, anchor)
    built, inner, outer = rim(False, keep_shares[0], inner_in, up_in, tiles_up, common, built, None)
    next_down = send_down(outer)
    built, inner, outer = rim(True, keep_shares[0], inner_in, down_in, tiles_down, common, built, inner)
    next_up = send_up(outer)
    up_in, down_in, inner_in = next_up, next_down, swap_inner(inner)

    def inside_operands(coded, thickness, tracer, velocity):
        return (
            coded, velocity, anchor[2], levels, gradient, average, edge_sources,
            thickness, tracer, anchor[0], anchor[1], divergence, cell_sources,
        )

    common = operands(built[1], built[2:5])
    built = call(
        whole_inside, keep_shares[1], inside_operands(*common[:4]), built_shapes, [vmem] * 5, [], "inside"
    )
    fluxes = call(tick, 0.0, (down_in,), (), [], [], "tick", passed=built[0])[0]
    built = (fluxes, *built[1:])
    built, inner, outer = rim(True, keep_shares[1], inner_in, down_in, tiles_down, common, built, None)
    next_up = send_up(outer)
    middle, near_middle = range(3, own - 3), range(4, own - 4)
    inner, fluxes, new_velocity, h, s = call(
        functools.partial(inside, EVEN, middle, near_middle), keep_shares[2], inside_operands(*built[1:]),
        (flux_shape, field_shapes[2]) + field_shapes[:2], [vmem] * 4, [], "even_middle", passed=inner,
    )
    built, inner, outer = rim(False, keep_shares[1], inner_in, up_in, tiles_up, common, built, inner)

    common = operands(built[1], built[2:5])
    outer, fluxes, new_velocity, h, s = call(
        functools.partial(inside, (3,), None, None), keep_shares[2], inside_operands(*common[:4]),
        (), [], [], "odd_inside", passed=outer, filled=(fluxes, new_velocity, h, s),
    )
    up_in, down_in = next_up, send_down(outer)

    far_shapes = (pltpu.HBM((LEV, cells), F32), pltpu.HBM((LEV, cells), F32), pltpu.HBM((LEV, edges), F32))
    inner, fluxes, new_velocity, h, s = call(
        functools.partial(inside, (1, 5, 7), None, None), keep_shares[2], inside_operands(*common[:4]),
        (), [], [], "odd_inside", passed=inner, filled=(fluxes, new_velocity, h, s),
    )
    inner_in = swap_inner(inner)
    fluxes = call(tick, 0.0, (up_in,), (), [], [], "tick", passed=fluxes)[0]
    edge_rest = [b for b in range(1, own - 1) if b not in middle]
    cell_rest = [b for b in range(2, own - 2) if b not in near_middle]
    fluxes, new_velocity, h, s = call(
        functools.partial(inside, EVEN, edge_rest, cell_rest), keep_shares[2], inside_operands(*common[:4]),
        (), [], [], "even_rest", filled=(fluxes, new_velocity, h, s),
    )
    h = call(tick, 0.0, (down_in,), (), [], [], "tick", passed=h)[0]
    results = pl.pallas_call(
        lambda *refs: last_rim_kernel(own, keep_shares[2], *refs),
        out_shape=(flux_shape,) + field_shapes + far_shapes,
        in_specs=[vmem] * 23,
        out_specs=[vmem] * 4 + [hbm] * 3,
        scratch_shapes=[pair_scratch, pltpu.SemaphoreType.DMA((9,))],
        input_output_aliases={19 + i: i for i in range(4)},
        compiler_params=params,
        cost_estimate=SMALL,
        name="rim",
    )(inner_in, up_in, down_in, tiles_inner, tiles_up, tiles_down, *common, fluxes, h, s, new_velocity)
    return results[4:]


def solution(mesh):
    return jax.shard_map(
        local,
        mesh=mesh,
        in_specs=(
            P(None, "dom"),
            P(None, "dom"),
            P(None, "dom"),
            P("dom"),
            P("dom", None, None, None),
            P("dom", None, None, None),
            P("dom", None),
            P("dom", None, None, None),
            P("dom", None),
        ),
        out_specs=(P(None, "dom"), P(None, "dom"), P(None, "dom")),
        check_vma=False,
    )
```

```python
import functools

import jax
import jax.numpy as jnp
from jax import lax
from jax.experimental import pallas as pl
from jax.experimental.pallas import tpu as pltpu
from jax.sharding import PartitionSpec as P

buoyancy = 0.2
drag_rate = 0.5
time_step = 0.25
keep_shares = (0.0, 0.75, 1.0 / 3.0)

F32 = jnp.float32
BF16 = jnp.bfloat16
LEV = 80
EVEN = (0, 2, 4, 6)
TILE = 128
SMALL = pl.CostEstimate(flops=1000, bytes_accessed=1000, transcendentals=0)
FIRST = pl.CostEstimate(flops=10**10, bytes_accessed=10**7, transcendentals=0)
LARGE = pl.CostEstimate(flops=10**9, bytes_accessed=10**6, transcendentals=0)
NEAR = 3 * LEV
NEXT = NEAR + 2 * LEV
MOVE = NEXT + 3 * LEV
SIDE = MOVE + 16


def lanes(block):
    return slice(block * TILE, (block + 1) * TILE)


def advance(anchor, current, slope, keep_share):
    if keep_share == 0.0:
        return current + time_step * slope
    return keep_share * anchor + (1.0 - keep_share) * (current + time_step * slope)


def block_mask(levels_ref, block):
    depth = lax.broadcasted_iota(jnp.int32, (LEV, TILE), 0)
    return (depth < levels_ref[block : block + 1, :]).astype(F32)


def above_weights():
    row = lax.broadcasted_iota(jnp.int32, (LEV, 3 * LEV), 0)
    column = lax.broadcasted_iota(jnp.int32, (LEV, 3 * LEV), 1)
    column = jnp.where(column >= 2 * LEV, column - 2 * LEV, jnp.where(column >= LEV, column - LEV, column))
    return jnp.where(column < row, 1.0, jnp.where(column == row, 0.5, 0.0)).astype(BF16)


def pressure_of(done, above):
    highs, middles, lows = [], [], []
    for thickness, tracer, mask in done:
        weight = thickness * (1.0 - buoyancy * tracer) * mask
        high = weight.astype(BF16)
        rest = weight - high.astype(F32)
        middle = rest.astype(BF16)
        highs.append(high)
        middles.append(middle)
        lows.append((rest - middle.astype(F32)).astype(BF16))
    parts = jnp.concatenate([jnp.concatenate(p, axis=1) for p in (highs, middles, lows)], axis=0)
    return jnp.dot(above, parts, preferred_element_type=F32) * (1.0 / LEV)


def code_blocks(coded, blocks, done, above):
    pressures = pressure_of(done, above)
    for i, (block, (thickness, tracer, mask)) in enumerate(zip(blocks, done)):
        coded[block, 0:LEV, :] = pressures[:, lanes(i)].astype(BF16)
        coded[block, LEV : 2 * LEV, :] = thickness.astype(BF16)
        coded[block, 2 * LEV : NEAR, :] = tracer.astype(BF16)


def edge_step(levels_mask, first, second, gradient, average, velocity, anchor, keep_share):
    slope = jnp.dot(
        jnp.concatenate([first[:LEV], second[:LEV]], axis=1), gradient, preferred_element_type=F32
    )
    carried = jnp.dot(
        jnp.concatenate([first[LEV:], second[LEV:]], axis=1), average, preferred_element_type=F32
    )
    moving = velocity * levels_mask
    flux = jnp.concatenate([carried[:LEV] * moving, carried[LEV:] * moving], axis=0).astype(BF16)
    change = (-slope - drag_rate * velocity) * levels_mask
    return flux, advance(anchor, velocity, change, keep_share)


def cell_step(block, fluxes_ref, sources_ref, first_block, own, whole, tiles_ref):
    picked = []
    for t in range(6):
        offset = sources_ref[t, block] - 3 * first_block
        offset = jnp.where(offset > 3 * own + 2, offset - 3 * whole, jnp.where(offset < -3, offset + 3 * whole, offset))
        picked.append(fluxes_ref[offset + 3])
    return -jnp.dot(jnp.concatenate(picked, axis=1), tiles_ref[block], preferred_element_type=F32)


def other_block(sources_ref, edge, first_block, own, whole):
    offset = sources_ref[1, edge] - first_block
    return jnp.where(offset > own, offset - whole, jnp.where(offset < -1, offset + whole, offset))


def start_kernel(
    own, thickness, tracer, velocity, levels, average, edge_sources, cell_sources,
    inner, outer, levels_out, edge_sources_out, cell_sources_out,
    h, s, v, flat, sems,
):
    position = lax.axis_index("dom")
    whole = own * lax.axis_size("dom")
    inner_side = 1 - lax.rem(position, 2)
    ends = []
    for p, side in ((0, inner_side), (1, 1 - inner_side)):
        block = side * (own - 1)
        ends.append((p, side, block, block + 1 - 2 * side))

    def columns(block, wide):
        return pl.ds(pl.multiple_of(block * TILE, TILE), wide)

    small = [
        pltpu.make_async_copy(levels, flat, sems.at[0]),
        pltpu.make_async_copy(edge_sources, edge_sources_out, sems.at[1]),
        pltpu.make_async_copy(cell_sources, cell_sources_out, sems.at[2]),
    ]
    fields, speeds, tiles = [], [], []
    for p, side, block, after in ends:
        for k, b in ((0, block), (1, after)):
            fields.append(pltpu.make_async_copy(thickness.at[:, columns(b, TILE)], h.at[p, k], sems.at[3 + 4 * p + 2 * k]))
            fields.append(pltpu.make_async_copy(tracer.at[:, columns(b, TILE)], s.at[p, k], sems.at[4 + 4 * p + 2 * k]))
        speeds.append(pltpu.make_async_copy(velocity.at[:, columns(3 * block, 3 * TILE)], v.at[p], sems.at[11 + p]))
        message = (inner, outer)[p]
        rows = pl.ds(pl.multiple_of(block * 6 * TILE, 6 * TILE), 6 * TILE)
        tiles.append(pltpu.make_async_copy(average.at[rows, :], message.at[pl.ds(SIDE, 6 * TILE), :], sems.at[13 + p]))
    for copy in small + fields + speeds + tiles:
        copy.start()
    above = above_weights()
    for copy in small:
        copy.wait()
    for block in range(own):
        levels_out[block] = flat[lanes(block)]
    for copy in fields:
        copy.wait()
    done = []
    for p, side, block, after in ends:
        depth = lax.broadcasted_iota(jnp.int32, (LEV, TILE), 0)
        done.append((h[p, 0], s[p, 0], (depth < levels_out[pl.ds(block, 1), :]).astype(F32)))
    pressures = pressure_of(done, above)
    for copy in speeds:
        copy.wait()
    for p, side, block, after in ends:
        message = (inner, outer)[p]
        mask = done[p][2]
        message[0:LEV, :] = pressures[:, lanes(p)].astype(BF16)
        message[LEV : 2 * LEV, :] = h[p, 0].astype(BF16)
        message[2 * LEV : NEAR, :] = s[p, 0].astype(BF16)
        message[NEAR : NEAR + LEV, :] = h[p, 1].astype(BF16)
        message[NEAR + LEV : NEXT, :] = s[p, 1].astype(BF16)
        row = lax.broadcasted_iota(jnp.int32, (16, TILE), 0)
        signs = jnp.zeros((16, TILE), F32)
        for j in range(3):
            message[NEXT + j * LEV : NEXT + (j + 1) * LEV, :] = (v[p, :, lanes(j)] * mask).astype(BF16)
            low = other_block(edge_sources_out, j, position * own, own, whole)
            high = other_block(edge_sources_out, 3 * (own - 1) + j, position * own, own, whole) - (own - 1)
            signs = jnp.where(row == j, jnp.where(side == 0, low, high).astype(F32), signs)
        message[MOVE:SIDE, :] = signs.astype(BF16)
    for copy in tiles:
        copy.wait()


def first_inside(
    own, keep_share, h0, s0, v0, levels, gradient, average, edge_sources, divergence, cell_sources,
    fluxes, new_coded, new_thickness, new_tracer, new_velocity, coded,
):
    done = [(h0[:, lanes(b)], s0[:, lanes(b)], block_mask(levels, b)) for b in range(own)]
    code_blocks(coded, range(own), done, above_weights())
    inside_edges(own, keep_share, coded, v0, v0, levels, gradient, average, edge_sources, fluxes, new_velocity)
    inside_cells(
        own, keep_share, fluxes, h0, s0, h0, s0, levels, divergence, cell_sources,
        new_coded, new_thickness, new_tracer,
    )


def on(places, work):
    place = lax.rem(lax.axis_index("dom"), 8)
    here = place == places[0]
    for other in places[1:]:
        here = here | (place == other)
    pl.when(here)(work)


def inside(
    places, edge_blocks, cell_blocks,
    own, keep_share, coded, velocity, velocity0, levels, gradient, average, edge_sources,
    thickness, tracer, thickness0, tracer0, divergence, cell_sources, *refs,
):
    fluxes, new_velocity, new_thickness, new_tracer = refs[-4:]

    def work():
        inside_edges(
            own, keep_share, coded, velocity, velocity0, levels, gradient, average, edge_sources, fluxes, new_velocity,
            edge_blocks,
        )
        inside_cells(
            own, keep_share, fluxes, thickness, tracer, thickness0, tracer0, levels, divergence, cell_sources,
            None, new_thickness, new_tracer, cell_blocks,
        )

    on(places, work)


def whole_inside(
    own, keep_share, coded, velocity, velocity0, levels, gradient, average, edge_sources,
    thickness, tracer, thickness0, tracer0, divergence, cell_sources,
    fluxes, new_coded, new_thickness, new_tracer, new_velocity,
):
    inside_edges(
        own, keep_share, coded, velocity, velocity0, levels, gradient, average, edge_sources, fluxes, new_velocity
    )
    inside_cells(
        own, keep_share, fluxes, thickness, tracer, thickness0, tracer0, levels, divergence, cell_sources,
        new_coded, new_thickness, new_tracer,
    )


def tick(own, keep_share, *refs):
    pass


def inside_edges(
    own, keep_share, coded, velocity, velocity0, levels, gradient, average, edge_sources, fluxes, new_velocity,
    blocks=None,
):
    whole = own * lax.axis_size("dom")
    first_block = lax.axis_index("dom") * own
    for block in blocks or range(1, own - 1):
        mask = block_mask(levels, block)
        for edge in range(3 * block, 3 * block + 3):
            other = other_block(edge_sources, edge, first_block, own, whole)
            flux, updated = edge_step(
                mask, coded[block], coded[other], gradient[edge], average[edge],
                velocity[:, lanes(edge)], velocity0[:, lanes(edge)], keep_share,
            )
            fluxes[edge + 3] = flux
            new_velocity[:, lanes(edge)] = updated


def inside_cells(
    own, keep_share, fluxes, thickness, tracer, thickness0, tracer0, levels, divergence, cell_sources,
    new_coded, new_thickness, new_tracer, blocks=None,
):
    whole = own * lax.axis_size("dom")
    first_block = lax.axis_index("dom") * own
    done = []
    for block in blocks or range(2, own - 2):
        done.append(
            finish_cell(
                block, own, keep_share, first_block, whole,
                thickness, tracer, thickness0, tracer0, levels, divergence, cell_sources,
                fluxes, new_thickness, new_tracer,
            )
        )
    if new_coded is not None:
        code_blocks(new_coded, range(2, own - 2), done, above_weights())


def finish_cell(
    block, own, keep_share, first_block, whole,
    thickness, tracer, thickness0, tracer0, levels, divergence, cell_sources,
    fluxes, new_thickness, new_tracer,
):
    at = lanes(block)
    mask = block_mask(levels, block)
    change = cell_step(block, fluxes, cell_sources, first_block, own, whole, divergence)
    h = advance(thickness0[:, at], thickness[:, at], change[:LEV] * mask, keep_share)
    s = advance(tracer0[:, at], tracer[:, at], change[LEV:] * mask, keep_share)
    new_thickness[:, at] = h
    new_tracer[:, at] = s
    return h, s, mask


def rim_step(
    odd, own, keep_share, last,
    outer_in, inner_in, tiles_outer, tiles_inner,
    coded, thickness, tracer, velocity, thickness0, tracer0, velocity0, levels,
    gradient, average, edge_sources, divergence, cell_sources,
    fluxes, new_coded, new_thickness, new_tracer, new_velocity, pair,
    inner, outer, send,
):
    above = above_weights()
    first_block = lax.axis_index("dom") * own
    whole = own * lax.axis_size("dom")
    halos = (inner_in, outer_in) if odd else (outer_in, inner_in)
    halo_tiles = (tiles_inner, tiles_outer) if odd else (tiles_outer, tiles_inner)
    messages = (inner, outer) if odd else (outer, inner)
    ends = ((0, 0, 1), (1, own - 1, own - 2))

    for side, block, after in ends:
        mask = block_mask(levels, block)
        outward = 2 * side - 1
        beyond = -1 if side == 0 else own
        halo, tiles = halos[side], halo_tiles[side]
        pair[side, 0] = halo[0:NEAR, :]
        pair[side, 1] = coded[after]
        signs = tiles[MOVE:SIDE, :].astype(F32)
        for j in range(3):
            edge = 3 * block + j
            other = other_block(edge_sources, edge, first_block, own, whole)
            flux, updated = edge_step(
                mask, coded[block], pair[side, (other == after).astype(jnp.int32)], gradient[edge], average[edge],
                velocity[:, lanes(edge)], velocity0[:, lanes(edge)], keep_share,
            )
            fluxes[edge + 3] = flux
            new_velocity[:, lanes(edge)] = updated
            toward = signs[j : j + 1, :] * outward
            second = jnp.where(
                jnp.broadcast_to(toward, (2 * LEV, TILE)) > 0.0,
                halo[NEAR:NEXT, :].astype(F32),
                coded[block, LEV:, :].astype(F32),
            ).astype(BF16)
            carried = jnp.dot(
                jnp.concatenate([halo[LEV:NEAR, :], second], axis=1),
                tiles[SIDE + j * 256 : SIDE + (j + 1) * 256, :],
                preferred_element_type=F32,
            )
            moving = halo[NEXT + j * LEV : NEXT + (j + 1) * LEV, :].astype(F32)
            fluxes[3 * beyond + 3 + j] = jnp.concatenate(
                [carried[:LEV] * moving, carried[LEV:] * moving], axis=0
            ).astype(BF16)
            if not last:
                messages[side][NEXT + j * LEV : NEXT + (j + 1) * LEV, :] = (updated * mask).astype(BF16)
        if last:
            send(2, 3 * block, 3)
    rim = (0, 1, own - 2, own - 1)
    done = []
    for block in rim:
        done.append(
            finish_cell(
                block, own, keep_share, first_block, whole,
                thickness, tracer, thickness0, tracer0, levels, divergence, cell_sources,
                fluxes, new_thickness, new_tracer,
            )
        )
        if last and block in (1, own - 1):
            send(0, block - 1, 2)
            send(1, block - 1, 2)
    if last:
        return
    code_blocks(new_coded, rim, done, above)
    for side, block, after in ends:
        messages[side][0:NEAR, :] = new_coded[block]
        messages[side][NEAR:NEXT, :] = new_coded[after, LEV:, :]


def rim_kernel(odd, second, own, keep_share, *refs):
    common = refs[:17]
    out = refs[17 + 5 + (1 if second else 0) :]
    built, inner, outer, pair = out[:5], out[5], out[6], out[7]

    @pl.when(lax.rem(lax.axis_index("dom"), 2) == (1 if odd else 0))
    def _():
        rim_step(odd, own, keep_share, False, *common, *built, pair, inner, outer, None)


def last_rim_kernel(own, keep_share, *refs):
    inner_in, up_in, down_in, tiles_inner, tiles_up, tiles_down = refs[:6]
    common = refs[6:19]
    fluxes, h, s, v, far_h, far_s, far_v, pair, sems = refs[23:]
    here, far = (h, s, v), (far_h, far_s, far_v)
    odd_here = lax.rem(lax.axis_index("dom"), 2)
    whole = []
    for which in (2, 0, 1):
        lo, wide = (3, 3 * (own - 2)) if which == 2 else (2, own - 4)
        at = (slice(None), pl.ds(lo * TILE, wide * TILE))
        whole.append(pltpu.make_async_copy(here[which].at[at], far[which].at[at], sems.at[which]))
        whole[-1].start()

    for odd in (False, True):

        @pl.when(odd_here == (1 if odd else 0))
        def _(odd=odd):
            sent = []

            def send(which, lo, wide):
                at = (slice(None), pl.ds(lo * TILE, wide * TILE))
                copy = pltpu.make_async_copy(here[which].at[at], far[which].at[at], sems.at[3 + len(sent)])
                copy.start()
                sent.append(copy)

            rim_step(
                odd, own, keep_share, True,
                down_in if odd else up_in, inner_in, tiles_down if odd else tiles_up, tiles_inner,
                *common, fluxes, None, h, s, v, pair, None, None, send,
            )
            for copy in sent:
                copy.wait()

    for copy in whole:
        copy.wait()


def in_vmem(array):
    return pltpu.with_memory_space_constraint(array, pltpu.VMEM)


def in_hbm(array):
    return pltpu.with_memory_space_constraint(array, pltpu.HBM)


def local(
    thickness,
    tracer,
    velocity,
    active_levels,
    gradient_tiles,
    average_tiles,
    edge_sources,
    divergence_tiles,
    cell_sources,
):
    own = cell_sources.shape[0]
    devices = lax.axis_size("dom")
    within = [(i, i ^ 1) for i in range(devices)]
    upward = [(i, (i + 1) % devices) for i in range(devices)]
    filler = {1: 1, 3: -3, 5: -1, 7: -1}
    downward = [(i, (i + filler[i % 8]) % devices if i % 2 else (i - 1) % devices) for i in range(devices)]
    cells, edges = thickness.shape[1], velocity.shape[1]
    vmem = pl.BlockSpec(memory_space=pltpu.VMEM)
    hbm = pl.BlockSpec(memory_space=pltpu.HBM)
    params = pltpu.CompilerParams(vmem_limit_bytes=16 * 1024 * 1024)

    gradient = (gradient_tiles.reshape(3 * own, 2 * TILE, TILE))
    average = (average_tiles.reshape(3 * own, 2 * TILE, TILE))
    average_rows = in_hbm(average_tiles.reshape(3 * own * 2 * TILE, TILE))
    divergence = (divergence_tiles.reshape(own, 6 * TILE, TILE))
    first_rows = SIDE + 6 * TILE

    def message(rows):
        return pltpu.VMEM((rows, TILE), BF16)

    inner, outer, levels, edge_sources, cell_sources = pl.pallas_call(
        lambda *refs: start_kernel(own, *refs),
        out_shape=(
            message(first_rows),
            message(first_rows),
            pltpu.VMEM((own, TILE), jnp.int32),
            pltpu.VMEM((2, 3 * own), jnp.int32),
            pltpu.VMEM((6, own), jnp.int32),
        ),
        in_specs=[hbm] * 7,
        out_specs=[vmem] * 5,
        scratch_shapes=[
            pltpu.VMEM((2, 2, LEV, TILE), F32),
            pltpu.VMEM((2, 2, LEV, TILE), F32),
            pltpu.VMEM((2, LEV, 3 * TILE), F32),
            pltpu.VMEM((cells,), jnp.int32),
            pltpu.SemaphoreType.DMA((15,)),
        ],
        compiler_params=params,
        cost_estimate=pl.CostEstimate(flops=2 * 10**10, bytes_accessed=10**6, transcendentals=0),
        name="start",
    )(in_hbm(thickness), in_hbm(tracer), in_hbm(velocity), in_hbm(active_levels), average_rows, in_hbm(edge_sources.T), in_hbm(cell_sources.T))

    coded_shape = pltpu.VMEM((own, NEAR, TILE), BF16)
    field_shapes = (
        pltpu.VMEM((LEV, cells), F32),
        pltpu.VMEM((LEV, cells), F32),
        pltpu.VMEM((LEV, edges), F32),
    )
    flux_shape = pltpu.VMEM((3 * own + 6, 2 * LEV, TILE), BF16)
    built_shapes = (flux_shape, coded_shape) + field_shapes
    pair_scratch = pltpu.VMEM((2, 2, NEAR, TILE), BF16)

    def send_up(x):
        return lax.ppermute(x, "dom", upward)

    def send_down(x):
        return lax.ppermute(x, "dom", downward)

    def swap_inner(x):
        return lax.ppermute(x, "dom", within)

    def rim(odd, keep_share, inner_in, outer_in, tiles_outer, common, built, inner):
        second = inner is not None
        extra = (inner,) if second else ()
        out = pl.pallas_call(
            lambda *refs: rim_kernel(odd, second, own, keep_share, *refs),
            out_shape=built_shapes + (message(MOVE), message(MOVE)),
            in_specs=[vmem] * (17 + 5 + len(extra)),
            out_specs=[vmem] * 7,
            scratch_shapes=[pair_scratch],
            input_output_aliases={17 + i: i for i in range(5 + len(extra))},
            compiler_params=params,
            cost_estimate=LARGE,
            name="rim_odd" if odd else "rim_even",
        )(outer_in, inner_in, tiles_outer, tiles_inner, *common, *built, *extra)
        return out[:5], out[5], out[6]

    def call(body, keep_share, operands, shapes, specs, scratch, name, after=None, passed=None, filled=()):
        n = len(operands)
        extra = tuple(x for x in (after, passed) if x is not None)
        given = tuple(x for x in (passed,) if x is not None) + filled
        total = n + len(extra) + len(filled)
        first = 0 if passed is None else 1
        return pl.pallas_call(
            lambda *refs: body(own, keep_share, *refs[:n], *refs[n + len(extra) : total], *refs[total + first :]),
            out_shape=tuple(pltpu.VMEM(x.shape, x.dtype) for x in given) + shapes,
            in_specs=[vmem] * total,
            out_specs=[vmem] * len(given) + specs,
            input_output_aliases={total - len(given) + i: i for i in range(len(given))},
            scratch_shapes=scratch,
            compiler_params=params,
            cost_estimate=FIRST if name == "first_inside" else SMALL,
            name=name,
        )(*operands, *extra, *filled)

    up_in, down_in = lax.ppermute(outer, "dom", upward), lax.ppermute(outer, "dom", [(j, i) for i, j in upward])
    anchor = (in_vmem(thickness), in_vmem(tracer), in_vmem(velocity))
    gradient, average, divergence = in_vmem(gradient), in_vmem(average), in_vmem(divergence)
    loaded = call(
        first_inside, keep_shares[0],
        (*anchor, levels, gradient, average, edge_sources, divergence, cell_sources),
        built_shapes + (coded_shape,), [vmem] * 6, [], "first_inside",
    )
    built, coded = loaded[:5], loaded[5]
    inner_in = swap_inner(inner)
    tiles_up, tiles_down, tiles_inner = up_in, down_in, inner_in

    def operands(coded, state):
        return (coded, *state, *anchor, levels, gradient, average, edge_sources, divergence, cell_sources)

    common = operands(coded, anchor)
    built, inner, outer = rim(False, keep_shares[0], inner_in, up_in, tiles_up, common, built, None)
    next_down = send_down(outer)
    built, inner, outer = rim(True, keep_shares[0], inner_in, down_in, tiles_down, common, built, inner)
    next_up = send_up(outer)
    up_in, down_in, inner_in = next_up, next_down, swap_inner(inner)

    def inside_operands(coded, thickness, tracer, velocity):
        return (
            coded, velocity, anchor[2], levels, gradient, average, edge_sources,
            thickness, tracer, anchor[0], anchor[1], divergence, cell_sources,
        )

    common = operands(built[1], built[2:5])
    built = call(
        whole_inside, keep_shares[1], inside_operands(*common[:4]), built_shapes, [vmem] * 5, [], "inside"
    )
    fluxes = call(tick, 0.0, (down_in,), (), [], [], "tick", passed=built[0])[0]
    built = (fluxes, *built[1:])
    built, inner, outer = rim(True, keep_shares[1], inner_in, down_in, tiles_down, common, built, None)
    next_up = send_up(outer)
    middle, near_middle = range(3, own - 3), range(4, own - 4)
    inner, fluxes, new_velocity, h, s = call(
        functools.partial(inside, EVEN, middle, near_middle), keep_shares[2], inside_operands(*built[1:]),
        (flux_shape, field_shapes[2]) + field_shapes[:2], [vmem] * 4, [], "even_middle", passed=inner,
    )
    built, inner, outer = rim(False, keep_shares[1], inner_in, up_in, tiles_up, common, built, inner)

    common = operands(built[1], built[2:5])
    outer, fluxes, new_velocity, h, s = call(
        functools.partial(inside, (3,), None, None), keep_shares[2], inside_operands(*common[:4]),
        (), [], [], "odd_inside", passed=outer, filled=(fluxes, new_velocity, h, s),
    )
    up_in, down_in = next_up, send_down(outer)

    far_shapes = (pltpu.HBM((LEV, cells), F32), pltpu.HBM((LEV, cells), F32), pltpu.HBM((LEV, edges), F32))
    inner, fluxes, new_velocity, h, s = call(
        functools.partial(inside, (1, 5, 7), None, None), keep_shares[2], inside_operands(*common[:4]),
        (), [], [], "odd_inside", passed=inner, filled=(fluxes, new_velocity, h, s),
    )
    inner_in = swap_inner(inner)
    fluxes = call(tick, 0.0, (up_in,), (), [], [], "tick", passed=fluxes)[0]
    edge_rest = [b for b in range(1, own - 1) if b not in middle]
    cell_rest = [b for b in range(2, own - 2) if b not in near_middle]
    fluxes, new_velocity, h, s = call(
        functools.partial(inside, EVEN, edge_rest, cell_rest), keep_shares[2], inside_operands(*common[:4]),
        (), [], [], "even_rest", filled=(fluxes, new_velocity, h, s),
    )
    h = call(tick, 0.0, (down_in,), (), [], [], "tick", passed=h)[0]
    results = pl.pallas_call(
        lambda *refs: last_rim_kernel(own, keep_shares[2], *refs),
        out_shape=(flux_shape,) + field_shapes + far_shapes,
        in_specs=[vmem] * 23,
        out_specs=[vmem] * 4 + [hbm] * 3,
        scratch_shapes=[pair_scratch, pltpu.SemaphoreType.DMA((9,))],
        input_output_aliases={19 + i: i for i in range(4)},
        compiler_params=params,
        cost_estimate=SMALL,
        name="rim",
    )(inner_in, up_in, down_in, tiles_inner, tiles_up, tiles_down, *common, fluxes, h, s, new_velocity)
    return results[4:]


def solution(mesh):
    return jax.shard_map(
        local,
        mesh=mesh,
        in_specs=(
            P(None, "dom"),
            P(None, "dom"),
            P(None, "dom"),
            P("dom"),
            P("dom", None, None, None),
            P("dom", None, None, None),
            P("dom", None),
            P("dom", None, None, None),
            P("dom", None),
        ),
        out_specs=(P(None, "dom"), P(None, "dom"), P(None, "dom")),
        check_vma=False,
    )
```
